256 devices in a mesh: gx: 8 (over z), gy: 8 (over x, core), gz: 4 (over y).
Axes of the slice: x: 4, y: 4, z: 8, core: 2. Of those that a mesh axis runs over, the one named last changes fastest.
Arguments:
- tri_geom: float32 [10, 2097152], P(None, ('gx', 'gy', 'gz')), as said below
- send_index: int32 [16384, 128], P(('gx', 'gy', 'gz')), may hold values from -1 to 8191, as said below
- near_index: int32 [64, 256, 512], P('gx', 'gy', 'gz'), may hold values from 0 to 8191, as said below
- return_cell: int32 [3, 2097152], P(None, ('gx', 'gy', 'gz')), may hold values from -1 to 32767, as said below
- velocity: float32 [3, 64, 256, 512], P(None, 'gx', 'gy', 'gz'), may hold values from -6 to 6
Outputs:
- new_velocity: float32 [3, 64, 256, 512], P(None, 'gx', 'gy', 'gz')
- indicator: float32 [64, 256, 512], P('gx', 'gy', 'gz')
- vertex_velocity: float32 [9, 2097152], P(None, ('gx', 'gy', 'gz'))
The draws below stay inside these ranges and needn't reach their ends.
Inputs may be any that keep to these rules, and one draw needn't show every extreme that they name: `send_index`: each row lists distinct local triangle indices of its owner in its first entries and -1 in the rest; every row has at least one triangle; an owner lists each of its triangles at most once over all its rows; for some bricks every owner fills all 128 slots. `near_index`: A value j * 128 + k names a slot that holds a triangle: k is below the number of triangles that owner j of the cell's row along gz lists for the cell's brick. `return_cell`: -1 where the vertex lies outside the brick. `tri_geom`: row 9 lies between 0.25 and 3.
All inputs are finite; a program needn't handle non-finite values.
Results may differ from the reference program's by a relative error of at most 0.0003.
Values sent between devices are 32-bit elements; how exact they have to be, the bound alone decides.
No kernel may reach another device: no remote copies, remote signals or barrier semaphores. Data moves between devices by JAX's collectives and lax.ppermute only.
A program may use at most 128 MiB of HBM per device.

```python
import jax
import jax.numpy as jnp
from jax import lax

BX = 8
BY = 32
BZ = 128
CAP = 128
NSWEEP = 4
BRICKS_X = 8
BRICKS_Y = 8
BRICKS_Z = 4
GROUP = 64
BRICKS = 256
TRI_DEV = 8192
TRIS = 2097152
SLOTS = 8192
CELLS = 32768
NX = 64
NY = 256
NZ = 512


def routing(key):
    key_hot, key_first, key_count = jax.random.split(jax.random.fold_in(key, 11), 3)
    is_hot = jax.random.randint(key_hot, (GROUP,), 0, 4) == 0
    first_hot = jax.random.randint(key_first, (), 0, GROUP)
    is_hot = is_hot | (jnp.arange(GROUP) == first_hot)
    counts = jnp.where(is_hot[None, :], CAP, jax.random.randint(key_count, (BRICKS, GROUP), 1, CAP + 1)).astype(jnp.int32)
    key_list = jax.random.split(jax.random.fold_in(key, 12), BRICKS)
    shuffled = jax.vmap(lambda subkey: jax.random.permutation(subkey, TRI_DEV))(key_list).astype(jnp.int32)
    offset = jnp.cumsum(counts, axis=1) - counts
    slot_ids = jnp.arange(CAP).astype(jnp.int32)
    position = offset[:, :, None] + slot_ids[None, None, :]
    filled = slot_ids[None, None, :] < counts[:, :, None]
    position = jnp.where(filled, position, 0)
    chosen = jnp.take_along_axis(shuffled, position.reshape(BRICKS, GROUP * CAP), axis=1).reshape(BRICKS, GROUP, CAP)
    return (counts, jnp.where(filled, chosen, -1).astype(jnp.int32))


def draw_send_index(key, part):
    counts, listed = routing(key)
    return listed.reshape(BRICKS * GROUP, CAP)


def draw_tri_geom(key, part):
    counts, listed = routing(key)
    rows = jnp.arange(BRICKS).astype(jnp.int32)[:, None, None]
    target = jnp.where(listed < 0, TRI_DEV, listed)
    dest_ids = jnp.broadcast_to(jnp.arange(GROUP).astype(jnp.int32)[None, :, None], listed.shape)
    dest = jnp.full((BRICKS, TRI_DEV + 1), -1, jnp.int32).at[rows, target].set(dest_ids)[:, :TRI_DEV]
    sent = dest >= 0
    safe_dest = jnp.maximum(dest, 0)
    row_z = (jnp.arange(BRICKS).astype(jnp.int32) % BRICKS_Z)[:, None]
    key_in, key_off, key_ten = jax.random.split(jax.random.fold_in(key, 13), 3)
    inside = jax.random.uniform(key_in, (3, BRICKS, TRI_DEV), jnp.float32)
    centre_x = jnp.where(sent, (safe_dest // BRICKS_Y * BX).astype(jnp.float32) + inside[0] * BX, inside[0] * NX)
    centre_y = jnp.where(sent, (safe_dest % BRICKS_Y * BY).astype(jnp.float32) + inside[1] * BY, inside[1] * NY)
    centre_z = jnp.where(sent, (row_z * BZ).astype(jnp.float32) + inside[2] * BZ, inside[2] * NZ)
    spread = 3.0
    tension = jnp.exp(jax.random.uniform(key_ten, (BRICKS, TRI_DEV), jnp.float32, jnp.log(0.5), jnp.log(2.0)))
    offsets = jax.random.normal(key_off, (9, BRICKS, TRI_DEV), jnp.float32) * spread
    centres = jnp.stack([centre_x, centre_y, centre_z] * 3)
    geometry = jnp.concatenate([centres + offsets, tension[None]], axis=0)
    return geometry.reshape(10, TRIS).astype(jnp.float32)


def draw_near_index(key, part):
    counts, listed = routing(key)
    grid_x = (jnp.arange(NX).astype(jnp.int32) // BX)[:, None, None]
    grid_y = (jnp.arange(NY).astype(jnp.int32) // BY)[None, :, None]
    grid_z = (jnp.arange(NZ).astype(jnp.int32) // BZ)[None, None, :]
    brick_row = grid_x * BRICKS_Y + grid_y
    key_src, key_slot = jax.random.split(jax.random.fold_in(key, 14))
    source = jax.random.randint(key_src, (NX, NY, NZ), 0, GROUP).astype(jnp.int32)
    owner = source * BRICKS_Z + grid_z
    limit = counts[owner, brick_row]
    within = jax.random.randint(key_slot, (NX, NY, NZ), 0, limit).astype(jnp.int32)
    return (source * CAP + within).astype(jnp.int32)


def draw_return_cell(key, part):
    key_out, key_cell = jax.random.split(jax.random.fold_in(key, 15))
    shape = (3, BRICKS * SLOTS)
    outside = jax.random.randint(key_out, shape, 0, 3) == 0
    return jnp.where(outside, -1, jax.random.randint(key_cell, shape, 0, CELLS)).astype(jnp.int32)


def shard_levels(own_key, extent, cuts, smallest, high):
    loudness, own = 1.0, jax.random.fold_in(own_key, 6)
    for axis_at, parts in cuts:
        steps = jnp.exp(jax.random.uniform(jax.random.fold_in(own, axis_at), (parts,), jnp.float32, smallest / len(cuts), high / len(cuts)))
        loudness = loudness * jnp.repeat(steps, extent[axis_at] // parts).reshape([-1 if axis == axis_at else 1 for axis in range(len(extent))])
    return loudness


def centred(own_key, extent, width, bound, cuts=(), dtype=jnp.bfloat16):
    gain = shard_levels(own_key, extent, cuts, -0.22, 0.18) if cuts else 1.0
    drawn = jax.random.normal(own_key, extent, jnp.float32) * width * gain
    return jnp.minimum(jnp.maximum(drawn, -bound), bound).astype(dtype)


def setup_inputs(seed: int = 0) -> dict:
    splits = jax.random.split(jax.random.key(seed), 6)
    tri_geom = draw_tri_geom(jax.random.fold_in(splits[5], 71), 0)
    send_index = draw_send_index(jax.random.fold_in(splits[5], 71), 0)
    near_index = draw_near_index(jax.random.fold_in(splits[5], 71), 0)
    return_cell = draw_return_cell(jax.random.fold_in(splits[5], 71), 0)
    velocity = centred(splits[4], (3, NX, NY, NZ), 1.0, 6.0, ((1, 8), (2, 8), (3, 4)), jnp.float32)
    return {"tri_geom": tri_geom, "send_index": send_index, "near_index": near_index, "return_cell": return_cell, "velocity": velocity}


time_step = 0.04
smear_width = 4.0
rho_liquid = 1.0
rho_gas = 0.05
mu_liquid = 2.0
mu_gas = 0.2

def brick_view(grid):
    leading = grid.shape[:-3]
    count = len(leading)
    shaped = grid.reshape(leading + (BRICKS_X, BX, BRICKS_Y, BY, BRICKS_Z, BZ))
    axes_order = tuple(range(count)) + (count, count + 2, count + 4, count + 1, count + 3, count + 5)
    return shaped.transpose(axes_order).reshape(leading + (BRICKS, CELLS))

def grid_view(blocks):
    leading = blocks.shape[:-2]
    count = len(leading)
    shaped = blocks.reshape(leading + (BRICKS_X, BRICKS_Y, BRICKS_Z, BX, BY, BZ))
    axes_order = tuple(range(count)) + (count, count + 3, count + 1, count + 4, count + 2, count + 5)
    return shaped.transpose(axes_order).reshape(leading + (NX, NY, NZ))

def slot_table(slots):
    first = slots[0:3]
    second = slots[3:6]
    third = slots[6:9]
    edge_one = second - first
    edge_two = third - first
    normal_x = edge_one[1] * edge_two[2] - edge_one[2] * edge_two[1]
    normal_y = edge_one[2] * edge_two[0] - edge_one[0] * edge_two[2]
    normal_z = edge_one[0] * edge_two[1] - edge_one[1] * edge_two[0]
    length = jnp.sqrt(normal_x * normal_x + normal_y * normal_y + normal_z * normal_z)
    scale = jnp.maximum(length, 1.0)
    centre = (first + second + third) / 3.0
    return jnp.stack([normal_x / scale, normal_y / scale, normal_z / scale, centre[0], centre[1], centre[2], slots[9]])

def reference(tri_geom, send_index, near_index, return_cell, velocity):
    owners = tri_geom.reshape(10, BRICKS, TRI_DEV)
    listed = send_index.reshape(BRICKS, GROUP * CAP)
    filled = listed >= 0
    gathered = jnp.take_along_axis(owners, jnp.maximum(listed, 0)[None], axis=2)
    gathered = jnp.where(filled[None], gathered, 0.0)
    received = gathered.reshape(10, GROUP, BRICKS_Z, GROUP, CAP).transpose(0, 3, 2, 1, 4).reshape(10, BRICKS, SLOTS)
    near_blocks = brick_view(near_index)
    brick_ids = jnp.arange(BRICKS).astype(jnp.int32)
    cell_ids = jnp.arange(CELLS).astype(jnp.int32)
    local_x = cell_ids // (BY * BZ)
    local_y = cell_ids // BZ % BY
    local_z = cell_ids % BZ

    def per_brick(packed):
        brick_id, slots, nearest = packed
        lookup = slot_table(slots)
        picked = jnp.take(lookup, nearest, axis=1)
        pos_x = (brick_id // (BRICKS_Y * BRICKS_Z) * BX + local_x).astype(jnp.float32) + 0.5
        pos_y = (brick_id // BRICKS_Z % BRICKS_Y * BY + local_y).astype(jnp.float32) + 0.5
        pos_z = (brick_id % BRICKS_Z * BZ + local_z).astype(jnp.float32) + 0.5
        distance = picked[0] * (pos_x - picked[3]) + picked[1] * (pos_y - picked[4]) + picked[2] * (pos_z - picked[5])
        return (0.5 * (1.0 + jnp.tanh(distance / smear_width)), picked[6])
    ind_blocks, ten_blocks = lax.map(per_brick, (brick_ids, received.transpose(1, 0, 2), near_blocks))
    indicator = grid_view(ind_blocks)
    tension = grid_view(ten_blocks)
    gradient = jnp.stack([(jnp.roll(indicator, -1, axis_id) - jnp.roll(indicator, 1, axis_id)) * 0.5 for axis_id in range(3)])
    density = rho_liquid + (rho_gas - rho_liquid) * indicator
    viscosity = mu_liquid + (mu_gas - mu_liquid) * indicator
    diffusion = viscosity / density
    forcing = tension * gradient / density
    current = velocity
    for repeat in range(NSWEEP):
        laplace = jnp.roll(current, -1, 1) + jnp.roll(current, 1, 1)
        laplace = laplace + jnp.roll(current, -1, 2) + jnp.roll(current, 1, 2)
        laplace = laplace + jnp.roll(current, -1, 3) + jnp.roll(current, 1, 3)
        laplace = laplace - 6.0 * current
        current = current + time_step * (diffusion * laplace + forcing)
    field_blocks = brick_view(current)
    cells_back = return_cell.reshape(3, BRICKS, SLOTS)
    samples = []
    for vertex in range(3):
        taken = jnp.take_along_axis(field_blocks, jnp.maximum(cells_back[vertex], 0)[None], axis=2)
        samples.append(jnp.where(cells_back[vertex][None] >= 0, taken, 0.0))
    sample = jnp.stack(samples, axis=1).reshape(9, BRICKS, SLOTS)
    back = sample.reshape(9, GROUP, BRICKS_Z, GROUP, CAP).transpose(0, 3, 2, 1, 4).reshape(9, BRICKS, GROUP * CAP)
    target = jnp.where(filled, listed, TRI_DEV)
    rows = jnp.arange(BRICKS).astype(jnp.int32)[:, None]
    vertex_velocity = jnp.zeros((9, BRICKS, TRI_DEV), jnp.float32).at[:, rows, target].add(back, mode='drop')
    return (current, indicator, vertex_velocity.reshape(9, TRIS))
```

```python
import jax
import jax.numpy as jnp
from jax import lax
from jax.experimental import pallas as pl
from jax.experimental.pallas import tpu as pltpu
from jax.sharding import PartitionSpec as P

NSWEEP = 4

time_step = 0.04
rho_liquid = 1.0
rho_gas = 0.05
mu_liquid = 2.0
mu_gas = 0.2

F32, BF16, I32 = jnp.float32, jnp.bfloat16, jnp.int32
LANE = 128
VMEM = pl.BlockSpec(memory_space=pltpu.VMEM)


def one_hot(rows, index):
    level = lax.broadcasted_iota(I32, (rows, index.shape[1]), 0)
    return jnp.where(level == index, 1.0, 0.0).astype(BF16)


def fold_lines(lines):
    sub = lax.broadcasted_iota(I32, (8, LANE), 0)
    step = 1
    while step < 8:
        low = (sub & step) == 0
        lines = [
            jnp.where(low, even, odd) + pltpu.roll(jnp.where(low, odd, even), step, 0)
            for even, odd in zip(lines[0::2], lines[1::2])
        ]
        step *= 2
    return lines[0]


def parts_of(value, count):
    out = []
    for _ in range(count - 1):
        head = value.astype(BF16)
        out.append(head)
        value = value - head.astype(F32)
    out.append(value.astype(BF16))
    return out


def put_table(table_ref, columns, halves):
    for q, column in enumerate(columns):
        table_ref[q * halves:(q + 1) * halves, 0:LANE] = column[0:halves]
        table_ref[q * halves:(q + 1) * halves, LANE:2 * LANE] = column[halves:2 * halves]


def look_up(table_ref, groups, half, lines):
    shift = half.bit_length() - 1
    tiles = half // 8
    sub = lax.broadcasted_iota(I32, (8, LANE), 0)
    count = sum(groups)
    found = [[] for _ in groups]
    for pair in range(4):
        index = jnp.concatenate([lines[2 * pair], lines[2 * pair + 1]], axis=1)
        row = index >> 7
        hot = one_hot(2 * LANE, ((row >> shift) << 7) + (index & 127))
        product = jnp.dot(table_ref[...], hot, preferred_element_type=F32)
        place = jnp.where(index < 0, -1, row & (half - 1))
        for side in range(2):
            here = place[:, side * LANE:(side + 1) * LANE]
            masks = [sub + 8 * t == here for t in range(tiles)]
            picked = []
            for q in range(count):
                total = jnp.zeros((8, LANE), F32)
                for t in range(tiles):
                    start = q * half + 8 * t
                    total = jnp.where(masks[t], product[start:start + 8, side * LANE:(side + 1) * LANE], total)
                picked.append(total)
            at = 0
            for g, size in enumerate(groups):
                total = picked[at]
                for other in picked[at + 1:at + size]:
                    total = total + other
                found[g].append(total)
                at += size
    return [fold_lines(column) for column in found]


def send_kernel(geom_ref, send_ref, origin_ref, out_ref, dense_ref, table_ref):
    rows = geom_ref.shape[1] // LANE
    half = rows // 2
    for h in range(rows):
        dense_ref[pl.ds(h, 10, stride=rows), :] = geom_ref[:, h * LANE:(h + 1) * LANE]
    geom = [dense_ref[r * rows:(r + 1) * rows, :] for r in range(10)]
    one = [geom[3 + a] - geom[a] for a in range(3)]
    two = [geom[6 + a] - geom[a] for a in range(3)]
    normal = [
        one[1] * two[2] - one[2] * two[1],
        one[2] * two[0] - one[0] * two[2],
        one[0] * two[1] - one[1] * two[0],
    ]
    length = jnp.sqrt(normal[0] * normal[0] + normal[1] * normal[1] + normal[2] * normal[2])
    scale = jnp.maximum(length, 1.0)
    columns = []
    offset = jnp.zeros_like(length)
    for a in range(3):
        head, tail = parts_of(normal[a] / scale, 2)
        columns += [head, tail]
        centre = (geom[a] + geom[3 + a] + geom[6 + a]) / 3.0 - origin_ref[a]
        offset = offset + (head.astype(F32) + tail.astype(F32)) * centre
    columns += parts_of(offset, 3) + parts_of(geom[9], 2)
    put_table(table_ref, columns, half)

    @pl.loop(0, send_ref.shape[0] // 8)
    def _(tile):
        index = send_ref[pl.ds(tile * 8, 8), :]
        found = look_up(table_ref, (2, 2, 2, 3, 2), half, [index[s:s + 1] for s in range(8)])
        for q, value in enumerate(found):
            out_ref[pl.ds(tile * 64 + q, 8, stride=8), :] = value


def send_tables(geom, send, origin):
    rows = geom.shape[1] // LANE
    dests = send.shape[0]
    return pl.pallas_call(
        send_kernel,
        name="send_tables",
        out_shape=jax.ShapeDtypeStruct((dests * 8, LANE), F32),
        in_specs=[VMEM, VMEM, pl.BlockSpec(memory_space=pltpu.SMEM)],
        out_specs=VMEM,
        scratch_shapes=[pltpu.VMEM((10 * rows, LANE), F32), pltpu.VMEM((11 * rows // 2, 2 * LANE), BF16)],
        compiler_params=pltpu.CompilerParams(vmem_limit_bytes=40 << 20),
        cost_estimate=pl.CostEstimate(flops=2 << 40, bytes_accessed=1 << 20, transcendentals=0),
    )(geom, send, origin)


def cell_kernel(tab_ref, near_ref, origin_ref, ind_ref, ten_ref, table_ref):
    sources = tab_ref.shape[0] // 8
    half = sources // 2
    size_x, size_y, _ = near_ref.shape
    value = [tab_ref[pl.ds(q, sources, stride=8), :] for q in range(5)]
    columns = []
    offset = value[3]
    for a in range(3):
        columns += parts_of(value[a], 2)
        offset = offset - value[a] * origin_ref[a]
    columns += parts_of(offset, 3) + parts_of(value[4], 2)
    put_table(table_ref, columns, half)
    mid_x, mid_y, mid_z = 0.5 * size_x, 0.5 * size_y, 0.5 * LANE
    sub = lax.broadcasted_iota(I32, (8, LANE), 0).astype(F32)
    at_z = lax.broadcasted_iota(I32, (8, LANE), 1).astype(F32) + (0.5 - mid_z)
    tiles = size_y // 8

    @pl.loop(0, size_x * tiles)
    def _(step):
        x = lax.shift_right_logical(step, tiles.bit_length() - 1)
        y = pl.multiple_of((step & (tiles - 1)) * 8, 8)
        index = near_ref[x, pl.ds(y, 8), :]
        found = look_up(table_ref, (2, 2, 2, 3, 2), half, [index[s:s + 1] for s in range(8)])
        at_x = x.astype(F32) + (0.5 - mid_x)
        at_y = sub + (y.astype(F32) + (0.5 - mid_y))
        distance = found[0] * at_x + found[1] * at_y + found[2] * at_z - found[3]
        ind_ref[x, pl.ds(y, 8), :] = 0.5 * (1.0 + jnp.tanh(distance / 4.0))
        ten_ref[x, pl.ds(y, 8), :] = found[4]


def cell_fields(tab, near, origin):
    sources = tab.shape[0] // 8
    out = jax.ShapeDtypeStruct(near.shape, F32)
    return pl.pallas_call(
        cell_kernel,
        name="cell_fields",
        out_shape=(out, out),
        in_specs=[VMEM, VMEM, pl.BlockSpec(memory_space=pltpu.SMEM)],
        out_specs=(VMEM, VMEM),
        scratch_shapes=[pltpu.VMEM((11 * sources // 2, 2 * LANE), BF16)],
        compiler_params=pltpu.CompilerParams(vmem_limit_bytes=40 << 20),
        cost_estimate=pl.CostEstimate(flops=6 << 40, bytes_accessed=1 << 20, transcendentals=0),
    )(tab, near, origin)


def vertex_kernel(field_ref, cell_ref, out_ref, table_ref):
    comps, rows, _ = field_ref.shape
    half = rows // 2
    columns = []
    for c in range(comps):
        columns += parts_of(field_ref[c], 2)
    put_table(table_ref, columns, half)
    sources = cell_ref.shape[1] // LANE

    @pl.loop(0, sources // 8)
    def _(tile):
        for v in range(3):
            lines = [
                cell_ref[v:v + 1, pl.ds(pl.multiple_of((tile * 8 + s) * LANE, LANE), LANE)] for s in range(8)
            ]
            found = look_up(table_ref, (2, 2, 2), half, lines)
            for c in range(3):
                out_ref[pl.ds(tile * 72 + 3 * c + v, 8, stride=9), :] = found[c]


def vertex_samples(field, cells):
    comps, rows, _ = field.shape
    sources = cells.shape[1] // LANE
    return pl.pallas_call(
        vertex_kernel,
        name="vertex_samples",
        out_shape=jax.ShapeDtypeStruct((sources * 9, LANE), F32),
        in_specs=[VMEM, VMEM],
        out_specs=VMEM,
        scratch_shapes=[pltpu.VMEM((6 * rows // 2, 2 * LANE), BF16)],
        compiler_params=pltpu.CompilerParams(vmem_limit_bytes=40 << 20),
        cost_estimate=pl.CostEstimate(flops=10 << 40, bytes_accessed=1 << 20, transcendentals=0),
    )(field, cells)


def home_kernel(back_ref, send_ref, out_ref, left_ref, right_ref, total_ref):
    dests = send_ref.shape[0]
    blocks = out_ref.shape[1] // (2 * LANE)
    chunk = left_ref.shape[1] // (2 * LANE)
    total_ref[...] = jnp.zeros_like(total_ref)

    @pl.loop(0, dests // chunk)
    def _(step):
        for line in range(chunk):
            d = step * chunk + line
            index = send_ref[pl.ds(d, 1), :]
            low = slice(line * LANE, (line + 1) * LANE)
            high = slice((chunk + line) * LANE, (chunk + line + 1) * LANE)
            hot = one_hot(2 * LANE, index & (2 * LANE - 1))
            right_ref[:, low] = hot
            right_ref[:, high] = hot
            mine = lax.broadcasted_iota(I32, (blocks, LANE), 0) == (index >> 8)
            for r in range(9):
                value = back_ref[pl.ds(d * 9 + r, 1), :]
                head = value.astype(BF16).astype(F32)
                tail = value - head
                rows = slice(r * blocks, (r + 1) * blocks)
                left_ref[rows, low] = jnp.where(mine, head, 0.0).astype(BF16)
                left_ref[rows, high] = jnp.where(mine, tail, 0.0).astype(BF16)
        total_ref[...] += lax.dot_general(
            left_ref[...], right_ref[...], (((1,), (1,)), ((), ())), preferred_element_type=F32
        )

    for r in range(9):
        for b in range(blocks):
            at = r * blocks + b
            out_ref[r:r + 1, b * 2 * LANE:(b + 1) * 2 * LANE] = total_ref[at:at + 1, :]


def bring_home(back, send, triangles):
    blocks = triangles // (2 * LANE)
    chunk = 4
    return pl.pallas_call(
        home_kernel,
        name="bring_home",
        out_shape=jax.ShapeDtypeStruct((9, triangles), F32),
        in_specs=[VMEM, VMEM],
        out_specs=VMEM,
        scratch_shapes=[
            pltpu.VMEM((9 * blocks, 2 * chunk * LANE), BF16),
            pltpu.VMEM((2 * LANE, 2 * chunk * LANE), BF16),
            pltpu.VMEM((9 * blocks, 2 * LANE), F32),
        ],
        compiler_params=pltpu.CompilerParams(vmem_limit_bytes=40 << 20),
        cost_estimate=pl.CostEstimate(flops=2 << 40, bytes_accessed=1 << 20, transcendentals=0),
    )(back, send)


def extended(cells, sides, width):
    for axis, dim in sides:
        count = lax.axis_size(axis)
        head = lax.slice_in_dim(cells, 0, width, axis=dim)
        tail = lax.slice_in_dim(cells, cells.shape[dim] - width, cells.shape[dim], axis=dim)
        cells = jnp.concatenate(
            [
                lax.ppermute(tail, axis, [(i, (i + 1) % count) for i in range(count)]),
                cells,
                lax.ppermute(head, axis, [((i + 1) % count, i) for i in range(count)]),
            ],
            axis=dim,
        )
    return cells


def coefficients(padded_ind, tension):
    gradient = jnp.stack(
        [
            (padded_ind[2:, 1:-1, 1:-1] - padded_ind[:-2, 1:-1, 1:-1]) * 0.5,
            (padded_ind[1:-1, 2:, 1:-1] - padded_ind[1:-1, :-2, 1:-1]) * 0.5,
            (padded_ind[1:-1, 1:-1, 2:] - padded_ind[1:-1, 1:-1, :-2]) * 0.5,
        ]
    )
    core_ind = padded_ind[1:-1, 1:-1, 1:-1]
    density = rho_liquid + (rho_gas - rho_liquid) * core_ind
    viscosity = mu_liquid + (mu_gas - mu_liquid) * core_ind
    return (viscosity / density, tension * gradient / density)


def stencil(padded):
    laplace = padded[:, 2:, 1:-1, 1:-1] + padded[:, :-2, 1:-1, 1:-1]
    laplace = laplace + padded[:, 1:-1, 2:, 1:-1] + padded[:, 1:-1, :-2, 1:-1]
    laplace = laplace + padded[:, 1:-1, 1:-1, 2:] + padded[:, 1:-1, 1:-1, :-2]
    return laplace - 6.0 * padded[:, 1:-1, 1:-1, 1:-1]


def per_device(tri_geom, send_index, near_index, return_cell, velocity):
    size_x, size_y, size_z = near_index.shape
    group_x, group_y = lax.axis_size("gx"), lax.axis_size("gy")
    mid_z = (lax.axis_index("gz") * size_z + size_z // 2).astype(F32)
    mid_x, mid_y = 0.5 * group_x * size_x, 0.5 * group_y * size_y
    outgoing = send_tables(tri_geom, send_index, jnp.stack([jnp.float32(mid_x), jnp.float32(mid_y), mid_z]))
    arrived = lax.all_to_all(
        outgoing.reshape(-1, 8, LANE), ("gx", "gy"), split_axis=0, concat_axis=0, tiled=True
    ).reshape(-1, LANE)
    own_x = (lax.axis_index("gx") * size_x + size_x // 2).astype(F32) - mid_x
    own_y = (lax.axis_index("gy") * size_y + size_y // 2).astype(F32) - mid_y
    indicator, tension = cell_fields(arrived, near_index, jnp.stack([own_x, own_y, jnp.float32(0.0)]))
    padded_ind = extended(indicator, (("gx", 0), ("gy", 1), ("gz", 2)), 1)
    diffusion, forcing = coefficients(padded_ind, tension)
    current = velocity
    for repeat in range(NSWEEP):
        padded = extended(current, (("gx", 1), ("gy", 2), ("gz", 3)), 1)
        laplace = stencil(padded)
        current = current + time_step * (diffusion * laplace + forcing)
    samples = vertex_samples(current.reshape(3, size_x * size_y, size_z), return_cell)
    returned = lax.all_to_all(
        samples.reshape(-1, 9 * LANE), ("gx", "gy"), split_axis=0, concat_axis=0, tiled=True
    ).reshape(-1, LANE)
    return (current, indicator, bring_home(returned, send_index, tri_geom.shape[1]))


def solution(mesh):
    placed = (
        P(None, ("gx", "gy", "gz")),
        P(("gx", "gy", "gz"), None),
        P("gx", "gy", "gz"),
        P(None, ("gx", "gy", "gz")),
        P(None, "gx", "gy", "gz"),
    )
    return jax.shard_map(
        per_device,
        mesh=mesh,
        in_specs=placed,
        out_specs=(P(None, "gx", "gy", "gz"), P("gx", "gy", "gz"), P(None, ("gx", "gy", "gz"))),
        check_vma=False,
    )
```

```python
import jax
import jax.numpy as jnp
from jax import lax
from jax.experimental import pallas as pl
from jax.experimental.pallas import tpu as pltpu
from jax.sharding import PartitionSpec as P

NSWEEP = 4
WIDE = NSWEEP

time_step = 0.04
smear_width = 4.0
rho_liquid = 1.0
rho_gas = 0.05
mu_liquid = 2.0
mu_gas = 0.2

F32, BF16, I32 = jnp.float32, jnp.bfloat16, jnp.int32
LANE = 128
VMEM = pl.BlockSpec(memory_space=pltpu.VMEM)


def one_hot(rows, index):
    level = lax.broadcasted_iota(I32, (rows, index.shape[1]), 0)
    return jnp.where(level == index, 1.0, 0.0).astype(BF16)


def fold_lines(lines):
    sub = lax.broadcasted_iota(I32, (8, LANE), 0)
    step = 1
    while step < 8:
        low = (sub & step) == 0
        lines = [
            jnp.where(low, even, odd) + pltpu.roll(jnp.where(low, odd, even), step, 0)
            for even, odd in zip(lines[0::2], lines[1::2])
        ]
        step *= 2
    return lines[0]


def parts_of(value, count):
    out = []
    for _ in range(count - 1):
        head = value.astype(BF16)
        out.append(head)
        value = value - head.astype(F32)
    out.append(value.astype(BF16))
    return out


def put_table(table_ref, columns, halves):
    for q, column in enumerate(columns):
        table_ref[q * halves:(q + 1) * halves, 0:LANE] = column[0:halves]
        table_ref[q * halves:(q + 1) * halves, LANE:2 * LANE] = column[halves:2 * halves]


def look_up(table_ref, groups, half, lines):
    shift = half.bit_length() - 1
    tiles = half // 8
    sub = lax.broadcasted_iota(I32, (8, LANE), 0)
    count = sum(groups)
    found = [[] for _ in groups]
    for pair in range(4):
        index = jnp.concatenate([lines[2 * pair], lines[2 * pair + 1]], axis=1)
        row = index >> 7
        hot = one_hot(2 * LANE, ((row >> shift) << 7) + (index & 127))
        product = jnp.dot(table_ref[...], hot, preferred_element_type=F32)
        place = jnp.where(index < 0, -1, row & (half - 1))
        for side in range(2):
            here = place[:, side * LANE:(side + 1) * LANE]
            masks = [sub + 8 * t == here for t in range(tiles)]
            picked = []
            for q in range(count):
                total = jnp.zeros((8, LANE), F32)
                for t in range(tiles):
                    start = q * half + 8 * t
                    total = jnp.where(masks[t], product[start:start + 8, side * LANE:(side + 1) * LANE], total)
                picked.append(total)
            at = 0
            for g, size in enumerate(groups):
                total = picked[at]
                for other in picked[at + 1:at + size]:
                    total = total + other
                found[g].append(total)
                at += size
    return [fold_lines(column) for column in found]


def send_kernel(geom_ref, send_ref, origin_ref, out_ref, dense_ref, table_ref):
    rows = geom_ref.shape[1] // LANE
    half = rows // 2
    for h in range(rows):
        dense_ref[pl.ds(h, 10, stride=rows), :] = geom_ref[:, h * LANE:(h + 1) * LANE]
    geom = [dense_ref[r * rows:(r + 1) * rows, :] for r in range(10)]
    one = [geom[3 + a] - geom[a] for a in range(3)]
    two = [geom[6 + a] - geom[a] for a in range(3)]
    normal = [
        one[1] * two[2] - one[2] * two[1],
        one[2] * two[0] - one[0] * two[2],
        one[0] * two[1] - one[1] * two[0],
    ]
    length = jnp.sqrt(normal[0] * normal[0] + normal[1] * normal[1] + normal[2] * normal[2])
    scale = jnp.maximum(length, 1.0)
    columns = []
    offset = jnp.zeros_like(length)
    for a in range(3):
        head, tail = parts_of(normal[a] / scale, 2)
        columns += [head, tail]
        centre = (geom[a] + geom[3 + a] + geom[6 + a]) / 3.0 - origin_ref[a]
        offset = offset + (head.astype(F32) + tail.astype(F32)) * centre
    columns += parts_of(offset, 3) + parts_of(geom[9], 2)
    put_table(table_ref, columns, half)

    @pl.loop(0, send_ref.shape[0] // 8)
    def _(tile):
        index = send_ref[pl.ds(tile * 8, 8), :]
        found = look_up(table_ref, (2, 2, 2, 3, 2), half, [index[s:s + 1] for s in range(8)])
        for q, value in enumerate(found):
            out_ref[pl.ds(tile * 64 + q, 8, stride=8), :] = value


def send_tables(geom, send, origin):
    rows = geom.shape[1] // LANE
    dests = send.shape[0]
    return pl.pallas_call(
        send_kernel,
        name="send_tables",
        out_shape=jax.ShapeDtypeStruct((dests * 8, LANE), F32),
        in_specs=[VMEM, VMEM, pl.BlockSpec(memory_space=pltpu.SMEM)],
        out_specs=VMEM,
        scratch_shapes=[pltpu.VMEM((10 * rows, LANE), F32), pltpu.VMEM((11 * rows // 2, 2 * LANE), BF16)],
        compiler_params=pltpu.CompilerParams(vmem_limit_bytes=40 << 20),
        cost_estimate=pl.CostEstimate(flops=2 << 40, bytes_accessed=1 << 20, transcendentals=0),
    )(geom, send, origin)


def cell_kernel(tab_ref, near_ref, origin_ref, ind_ref, low_ref, high_ref, table_ref):
    sources = tab_ref.shape[0] // 8
    half = sources // 2
    size_x, size_y, _ = near_ref.shape
    value = [tab_ref[pl.ds(q, sources, stride=8), :] for q in range(5)]
    columns = []
    offset = value[3]
    for a in range(3):
        columns += parts_of(value[a], 2)
        offset = offset - value[a] * origin_ref[a]
    columns += parts_of(offset, 3) + parts_of(value[4], 2)
    put_table(table_ref, columns, half)
    mid_x, mid_y, mid_z = 0.5 * size_x, 0.5 * size_y, 0.5 * LANE
    sub = lax.broadcasted_iota(I32, (8, LANE), 0).astype(F32)
    at_z = lax.broadcasted_iota(I32, (8, LANE), 1).astype(F32) + (0.5 - mid_z)
    tiles = size_y // 8

    @pl.loop(0, size_x * tiles)
    def _(step):
        x = lax.shift_right_logical(step, tiles.bit_length() - 1)
        y = pl.multiple_of((step & (tiles - 1)) * 8, 8)
        index = near_ref[x, pl.ds(y, 8), :]
        found = look_up(table_ref, (2, 2, 2, 3, 2), half, [index[s:s + 1] for s in range(8)])
        at_x = x.astype(F32) + (0.5 - mid_x)
        at_y = sub + (y.astype(F32) + (0.5 - mid_y))
        distance = found[0] * at_x + found[1] * at_y + found[2] * at_z - found[3]
        indicator = 0.5 * (1.0 + jnp.tanh(distance / smear_width))
        ind_ref[x, pl.ds(y, 8), :] = indicator

        @pl.when(x < WIDE)
        def _():
            low_ref[0, x, pl.ds(y, 8), :] = indicator
            low_ref[1, x, pl.ds(y, 8), :] = found[4]

        @pl.when(x >= WIDE)
        def _():
            high_ref[0, x - WIDE, pl.ds(y, 8), :] = indicator
            high_ref[1, x - WIDE, pl.ds(y, 8), :] = found[4]


def cell_fields(tab, near, origin):
    sources = tab.shape[0] // 8
    out = jax.ShapeDtypeStruct(near.shape, F32)
    side = jax.ShapeDtypeStruct((2, WIDE) + near.shape[1:], F32)
    return pl.pallas_call(
        cell_kernel,
        name="cell_fields",
        out_shape=(out, side, side),
        in_specs=[VMEM, VMEM, pl.BlockSpec(memory_space=pltpu.SMEM)],
        out_specs=(VMEM, VMEM, VMEM),
        scratch_shapes=[pltpu.VMEM((11 * sources // 2, 2 * LANE), BF16)],
        compiler_params=pltpu.CompilerParams(vmem_limit_bytes=40 << 20),
        cost_estimate=pl.CostEstimate(flops=6 << 40, bytes_accessed=1 << 20, transcendentals=0),
    )(tab, near, origin)


def vertex_kernel(field_ref, cell_ref, out_ref, table_ref):
    comps, rows, _ = field_ref.shape
    half = rows // 2
    columns = []
    for c in range(comps):
        columns += parts_of(field_ref[c], 2)
    put_table(table_ref, columns, half)
    sources = cell_ref.shape[1] // LANE

    @pl.loop(0, sources // 8)
    def _(tile):
        for v in range(3):
            lines = [
                cell_ref[v:v + 1, pl.ds(pl.multiple_of((tile * 8 + s) * LANE, LANE), LANE)] for s in range(8)
            ]
            found = look_up(table_ref, (2, 2, 2), half, lines)
            for c in range(3):
                out_ref[pl.ds(tile * 72 + 3 * c + v, 8, stride=9), :] = found[c]


def vertex_samples(field, cells):
    comps, rows, _ = field.shape
    sources = cells.shape[1] // LANE
    return pl.pallas_call(
        vertex_kernel,
        name="vertex_samples",
        out_shape=jax.ShapeDtypeStruct((sources * 9, LANE), F32),
        in_specs=[VMEM, VMEM],
        out_specs=VMEM,
        scratch_shapes=[pltpu.VMEM((6 * rows // 2, 2 * LANE), BF16)],
        compiler_params=pltpu.CompilerParams(vmem_limit_bytes=40 << 20),
        cost_estimate=pl.CostEstimate(flops=10 << 40, bytes_accessed=1 << 20, transcendentals=0),
    )(field, cells)


def home_kernel(back_ref, send_ref, out_ref, left_ref, right_ref, total_ref):
    dests = send_ref.shape[0]
    blocks = out_ref.shape[1] // (2 * LANE)
    chunk = left_ref.shape[1] // (2 * LANE)
    total_ref[...] = jnp.zeros_like(total_ref)

    @pl.loop(0, dests // chunk)
    def _(step):
        for line in range(chunk):
            d = step * chunk + line
            index = send_ref[pl.ds(d, 1), :]
            low = slice(line * LANE, (line + 1) * LANE)
            high = slice((chunk + line) * LANE, (chunk + line + 1) * LANE)
            hot = one_hot(2 * LANE, index & (2 * LANE - 1))
            right_ref[:, low] = hot
            right_ref[:, high] = hot
            mine = lax.broadcasted_iota(I32, (blocks, LANE), 0) == (index >> 8)
            for r in range(9):
                value = back_ref[pl.ds(d * 9 + r, 1), :]
                head = value.astype(BF16).astype(F32)
                tail = value - head
                rows = slice(r * blocks, (r + 1) * blocks)
                left_ref[rows, low] = jnp.where(mine, head, 0.0).astype(BF16)
                left_ref[rows, high] = jnp.where(mine, tail, 0.0).astype(BF16)
        total_ref[...] += lax.dot_general(
            left_ref[...], right_ref[...], (((1,), (1,)), ((), ())), preferred_element_type=F32
        )

    for r in range(9):
        for b in range(blocks):
            at = r * blocks + b
            out_ref[r:r + 1, b * 2 * LANE:(b + 1) * 2 * LANE] = total_ref[at:at + 1, :]


def bring_home(back, send, triangles):
    blocks = triangles // (2 * LANE)
    chunk = 4
    return pl.pallas_call(
        home_kernel,
        name="bring_home",
        out_shape=jax.ShapeDtypeStruct((9, triangles), F32),
        in_specs=[VMEM, VMEM],
        out_specs=VMEM,
        scratch_shapes=[
            pltpu.VMEM((9 * blocks, 2 * chunk * LANE), BF16),
            pltpu.VMEM((2 * LANE, 2 * chunk * LANE), BF16),
            pltpu.VMEM((9 * blocks, 2 * LANE), F32),
        ],
        compiler_params=pltpu.CompilerParams(vmem_limit_bytes=40 << 20),
        cost_estimate=pl.CostEstimate(flops=2 << 40, bytes_accessed=1 << 20, transcendentals=0),
    )(back, send)


def pack_y_kernel(low_ref, high_ref, below_ref, above_ref, down_ref, up_ref):
    size_y = low_ref.shape[2]
    at = 0
    for c in range(low_ref.shape[0]):
        for ref in (below_ref, low_ref, high_ref, above_ref):
            for x in range(WIDE):
                down_ref[at:at + WIDE, :] = ref[c, x, 0:WIDE, :]
                up_ref[at:at + WIDE, :] = ref[c, x, size_y - WIDE:size_y, :]
                at += WIDE


def pack_y(low, high, below, above):
    out = jax.ShapeDtypeStruct((low.shape[0] * 4 * WIDE * WIDE, LANE), F32)
    return pl.pallas_call(
        pack_y_kernel,
        name="pack_y",
        out_shape=(out, out),
        in_specs=[VMEM] * 4,
        out_specs=(VMEM, VMEM),
        compiler_params=pltpu.CompilerParams(vmem_limit_bytes=16 << 20),
        cost_estimate=pl.CostEstimate(flops=1 << 20, bytes_accessed=1 << 20, transcendentals=0),
    )(low, high, below, above)


def pack_z_kernel(*refs):
    wide_ref, down_ref, up_ref = refs[-3:]
    lane = lax.broadcasted_iota(I32, (1, LANE), 1)
    group = lax.shift_right_logical(lane, 2)
    size_y = refs[0].shape[2]
    field = 0
    down = up = None
    for low_ref, high_ref, below_ref, above_ref, under_ref, over_ref in (refs[0:6], refs[6:12]):
        at = 0
        for c in range(low_ref.shape[0]):
            side = field % 2
            if side == 0:
                down = jnp.zeros((size_y + 2 * WIDE, LANE), F32)
                up = jnp.zeros((size_y + 2 * WIDE, LANE), F32)
            x = 0
            for ref in (below_ref, low_ref, high_ref, above_ref):
                for k in range(WIDE):
                    plane = jnp.concatenate(
                        [ref[c, k], over_ref[at:at + WIDE, :], under_ref[at:at + WIDE, :]], axis=0
                    )
                    wide_ref[field, x] = plane
                    slot = x + 4 * WIDE * side
                    here = group == slot
                    shift = WIDE * slot
                    moved = pltpu.roll(plane, shift, 1) if shift else plane
                    down = jnp.where(here, moved, down)
                    shift = (shift + WIDE) % LANE
                    moved = pltpu.roll(plane, shift, 1) if shift else plane
                    up = jnp.where(here, moved, up)
                    at += WIDE
                    x += 1
            rows = pl.ds((field // 2) * (size_y + 2 * WIDE), size_y + 2 * WIDE)
            down_ref[rows, :] = down
            up_ref[rows, :] = up
            field += 1


def pack_z(first, second):
    fields = first[0].shape[0] + second[0].shape[0]
    rows = first[0].shape[2] + 2 * WIDE
    message = jax.ShapeDtypeStruct(((fields + 1) // 2 * rows, LANE), F32)
    return pl.pallas_call(
        pack_z_kernel,
        name="pack_z",
        out_shape=(jax.ShapeDtypeStruct((fields, 4 * WIDE, rows, LANE), F32), message, message),
        in_specs=[VMEM] * 12,
        out_specs=(VMEM,) * 3,
        compiler_params=pltpu.CompilerParams(vmem_limit_bytes=24 << 20),
        cost_estimate=pl.CostEstimate(flops=1 << 20, bytes_accessed=1 << 20, transcendentals=0),
    )(*first, *second)


def sweep_kernel(wide_ref, before_ref, after_ref, out_ref, one_ref, two_ref, coef_ref):
    rows = wide_ref.shape[2]
    planes = wide_ref.shape[1]
    size_x = planes - 2 * WIDE
    size_y = rows - 2 * WIDE
    lane = lax.broadcasted_iota(I32, (rows, LANE), 1)
    first, last = lane == 0, lane == LANE - 1
    main, rim = slice(0, rows), slice(rows, 2 * rows)
    for field in range(5):
        pair = slice((field // 2) * rows, (field // 2 + 1) * rows)
        after, before = after_ref[pair, :], before_ref[pair, :]
        for x in range(planes):
            shift = WIDE * (x + planes * (field % 2))
            near = pltpu.roll(after, (LANE - shift) % LANE, 1) if shift else after
            far = pltpu.roll(before, LANE - WIDE - shift, 1) if LANE - WIDE - shift else before
            edge = jnp.where(lane < WIDE, near, jnp.where(lane >= LANE - WIDE, far, 0.0))
            one_ref[field, x, main] = wide_ref[field, x]
            one_ref[field, x, rim] = edge

    def along_z(middle, edge):
        m, e = pltpu.roll(middle, LANE - 1, 1), pltpu.roll(edge, LANE - 1, 1)
        next_m, next_e = jnp.where(last, e, m), jnp.where(last, m, e)
        m, e = pltpu.roll(middle, 1, 1), pltpu.roll(edge, 1, 1)
        return next_m, next_e, jnp.where(first, e, m), jnp.where(first, m, e)

    @pl.loop(1, planes - 1)
    def _(x):
        ind = [one_ref[3, x, main], one_ref[3, x, rim]]
        next_m, next_e, prev_m, prev_e = along_z(ind[0], ind[1])
        for at, centre, along in ((main, ind[0], next_m - prev_m), (rim, ind[1], next_e - prev_e)):
            density = rho_liquid + (rho_gas - rho_liquid) * centre
            viscosity = mu_liquid + (mu_gas - mu_liquid) * centre
            scale = time_step / density
            pull = one_ref[4, x, at] * scale * 0.5
            coef_ref[0, x, at] = viscosity * scale
            coef_ref[1, x, at] = pull * (one_ref[3, x + 1, at] - one_ref[3, x - 1, at])
            coef_ref[2, x, at] = pull * (pltpu.roll(centre, rows - 1, 0) - pltpu.roll(centre, 1, 0))
            coef_ref[3, x, at] = pull * along

    def sweep(source, margin, store):
        @pl.loop(WIDE - margin, planes - WIDE + margin)
        def _(x):
            for c in range(3):
                middle, edge = source[c, x, main], source[c, x, rim]
                next_m, next_e, prev_m, prev_e = along_z(middle, edge)
                parts = [(main, middle, next_m + prev_m)]
                if margin:
                    parts.append((rim, edge, next_e + prev_e))
                for at, centre, along in parts:
                    laplace = source[c, x + 1, at] + source[c, x - 1, at]
                    laplace = laplace + pltpu.roll(centre, rows - 1, 0) + pltpu.roll(centre, 1, 0)
                    laplace = laplace + along - 6.0 * centre
                    store(c, x, at, centre + (coef_ref[0, x, at] * laplace + coef_ref[1 + c, x, at]))

    def into(ref):
        def store(c, x, at, value):
            ref[c, x, at] = value
        return store

    def into_result(c, x, at, value):
        out_ref[c, x - WIDE] = value[0:size_y]

    sweep(one_ref, 3, into(two_ref))
    sweep(two_ref, 2, into(one_ref))
    sweep(one_ref, 1, into(two_ref))
    sweep(two_ref, 0, into_result)


def swept(wide, before, after):
    _, planes, rows, _ = wide.shape
    return pl.pallas_call(
        sweep_kernel,
        name="sweeps",
        out_shape=jax.ShapeDtypeStruct((3, planes - 2 * WIDE, rows - 2 * WIDE, LANE), F32),
        in_specs=[VMEM] * 3,
        out_specs=VMEM,
        scratch_shapes=[
            pltpu.VMEM((5, planes, 2 * rows, LANE), F32),
            pltpu.VMEM((3, planes, 2 * rows, LANE), F32),
            pltpu.VMEM((4, planes, 2 * rows, LANE), F32),
        ],
        compiler_params=pltpu.CompilerParams(vmem_limit_bytes=40 << 20),
        cost_estimate=pl.CostEstimate(flops=1 << 30, bytes_accessed=1 << 20, transcendentals=0),
    )(wide, before, after)


def both_ways(down, up, axis):
    count = lax.axis_size(axis)
    above = lax.ppermute(down, axis, [((i + 1) % count, i) for i in range(count)])
    below = lax.ppermute(up, axis, [(i, (i + 1) % count) for i in range(count)])
    return below, above


def per_device(tri_geom, send_index, near_index, return_cell, velocity):
    size_x, size_y, size_z = near_index.shape
    group_x, group_y = lax.axis_size("gx"), lax.axis_size("gy")
    vel_low, vel_high = velocity[:, :WIDE], velocity[:, WIDE:]
    vel_below, vel_above = both_ways(vel_low, vel_high, "gx")
    mid_z = (lax.axis_index("gz") * size_z + size_z // 2).astype(F32)
    mid_x, mid_y = 0.5 * group_x * size_x, 0.5 * group_y * size_y
    outgoing = send_tables(tri_geom, send_index, jnp.stack([jnp.float32(mid_x), jnp.float32(mid_y), mid_z]))
    arrived = lax.all_to_all(
        outgoing.reshape(-1, 8, LANE), ("gx", "gy"), split_axis=0, concat_axis=0, tiled=True
    ).reshape(-1, LANE)
    vel_down, vel_up = pack_y(vel_low, vel_high, vel_below, vel_above)
    vel_under, vel_over = both_ways(vel_down, vel_up, "gy")
    own_x = (lax.axis_index("gx") * size_x + size_x // 2).astype(F32) - mid_x
    own_y = (lax.axis_index("gy") * size_y + size_y // 2).astype(F32) - mid_y
    indicator, low, high = cell_fields(arrived, near_index, jnp.stack([own_x, own_y, jnp.float32(0.0)]))
    below, above = both_ways(low, high, "gx")
    down, up = pack_y(low, high, below, above)
    under, over = both_ways(down, up, "gy")
    wide, down, up = pack_z(
        (vel_low, vel_high, vel_below, vel_above, vel_under, vel_over), (low, high, below, above, under, over)
    )
    before, after = both_ways(down, up, "gz")
    current = swept(wide, before, after)
    samples = vertex_samples(current.reshape(3, size_x * size_y, size_z), return_cell)
    returned = lax.all_to_all(
        samples.reshape(-1, 9 * LANE), ("gx", "gy"), split_axis=0, concat_axis=0, tiled=True
    ).reshape(-1, LANE)
    return (current, indicator, bring_home(returned, send_index, tri_geom.shape[1]))


def solution(mesh):
    placed = (
        P(None, ("gx", "gy", "gz")),
        P(("gx", "gy", "gz"), None),
        P("gx", "gy", "gz"),
        P(None, ("gx", "gy", "gz")),
        P(None, "gx", "gy", "gz"),
    )
    return jax.shard_map(
        per_device,
        mesh=mesh,
        in_specs=placed,
        out_specs=(P(None, "gx", "gy", "gz"), P("gx", "gy", "gz"), P(None, ("gx", "gy", "gz"))),
        check_vma=False,
    )
```

```python
import jax
import jax.numpy as jnp
from jax import lax
from jax.experimental import pallas as pl
from jax.experimental.pallas import tpu as pltpu
from jax.sharding import PartitionSpec as P

NSWEEP = 4
WIDE = NSWEEP

time_step = 0.04
smear_width = 4.0
rho_liquid = 1.0
rho_gas = 0.05
mu_liquid = 2.0
mu_gas = 0.2

F32, BF16, I32 = jnp.float32, jnp.bfloat16, jnp.int32
LANE = 128
SPAN = 2
VMEM = pl.BlockSpec(memory_space=pltpu.VMEM)


def one_hot(rows, index):
    level = lax.broadcasted_iota(I32, (rows, index.shape[1]), 0).astype(F32).astype(BF16)
    same = level == index.astype(F32).astype(BF16)
    return jnp.where(same, jnp.ones_like(level), jnp.zeros_like(level))


def fold_lines(lines):
    sub = lax.broadcasted_iota(I32, (8, LANE), 0)
    step = 1
    while step < 8:
        low = (sub & step) == 0
        lines = [
            jnp.where(low, even, odd) + pltpu.roll(jnp.where(low, odd, even), step, 0)
            for even, odd in zip(lines[0::2], lines[1::2])
        ]
        step *= 2
    return lines[0]


def parts_of(value, count):
    out = []
    for _ in range(count - 1):
        head = value.astype(BF16)
        out.append(head)
        value = value - head.astype(F32)
    out.append(value.astype(BF16))
    return out


def put_table(table_ref, columns, halves):
    for q, column in enumerate(columns):
        table_ref[q * halves:(q + 1) * halves, 0:LANE] = column[0:halves]
        table_ref[q * halves:(q + 1) * halves, LANE:2 * LANE] = column[halves:2 * halves]


def look_up(table_ref, groups, half, lines):
    shift = half.bit_length() - 1
    tiles = half // 8
    sub = lax.broadcasted_iota(I32, (8, LANE), 0)
    count = sum(groups)
    found = [[] for _ in groups]
    for pair in range(8 // SPAN):
        index = jnp.concatenate(lines[SPAN * pair:SPAN * (pair + 1)], axis=1)
        row = index >> 7
        hot = one_hot(2 * LANE, ((row >> shift) << 7) + (index & 127))
        product = jnp.dot(table_ref[...], hot, preferred_element_type=F32)
        place = jnp.where(index < 0, -1, row & (half - 1))
        for side in range(SPAN):
            here = place[:, side * LANE:(side + 1) * LANE]
            masks = [sub + 8 * t == here for t in range(tiles)]
            picked = []
            for q in range(count):
                total = jnp.zeros((8, LANE), F32)
                for t in range(tiles):
                    start = q * half + 8 * t
                    total = jnp.where(masks[t], product[start:start + 8, side * LANE:(side + 1) * LANE], total)
                picked.append(total)
            at = 0
            for g, size in enumerate(groups):
                total = picked[at]
                for other in picked[at + 1:at + size]:
                    total = total + other
                found[g].append(total)
                at += size
    return [fold_lines(column) for column in found]


def send_kernel(geom_ref, send_ref, origin_ref, out_ref, dense_ref, table_ref):
    rows = geom_ref.shape[1] // LANE
    half = rows // 2
    for h in range(rows):
        dense_ref[pl.ds(h, 10, stride=rows), :] = geom_ref[:, h * LANE:(h + 1) * LANE]
    geom = [dense_ref[r * rows:(r + 1) * rows, :] for r in range(10)]
    one = [geom[3 + a] - geom[a] for a in range(3)]
    two = [geom[6 + a] - geom[a] for a in range(3)]
    normal = [
        one[1] * two[2] - one[2] * two[1],
        one[2] * two[0] - one[0] * two[2],
        one[0] * two[1] - one[1] * two[0],
    ]
    length = jnp.sqrt(normal[0] * normal[0] + normal[1] * normal[1] + normal[2] * normal[2])
    scale = jnp.maximum(length, 1.0)
    columns = []
    offset = jnp.zeros_like(length)
    for a in range(3):
        head, tail = parts_of(normal[a] / scale, 2)
        columns += [head, tail]
        centre = (geom[a] + geom[3 + a] + geom[6 + a]) / 3.0 - origin_ref[a]
        offset = offset + (head.astype(F32) + tail.astype(F32)) * centre
    columns += parts_of(offset, 3) + parts_of(geom[9], 2)
    put_table(table_ref, columns, half)

    @pl.loop(0, send_ref.shape[0] // 8, unroll=8)
    def _(tile):
        index = send_ref[pl.ds(tile * 8, 8), :]
        found = look_up(table_ref, (2, 2, 2, 3, 2), half, [index[s:s + 1] for s in range(8)])
        for q, value in enumerate(found):
            out_ref[pl.ds(tile * 64 + q, 8, stride=8), :] = value


def send_tables(geom, send, origin):
    rows = geom.shape[1] // LANE
    dests = send.shape[0]
    return pl.pallas_call(
        send_kernel,
        name="send_tables",
        out_shape=jax.ShapeDtypeStruct((dests * 8, LANE), F32),
        in_specs=[VMEM, VMEM, pl.BlockSpec(memory_space=pltpu.SMEM)],
        out_specs=VMEM,
        scratch_shapes=[pltpu.VMEM((10 * rows, LANE), F32), pltpu.VMEM((11 * rows // 2, 2 * LANE), BF16)],
        compiler_params=pltpu.CompilerParams(vmem_limit_bytes=40 << 20),
        cost_estimate=pl.CostEstimate(flops=2 << 40, bytes_accessed=1 << 20, transcendentals=0),
    )(geom, send, origin)


def cell_kernel(tab_ref, near_ref, origin_ref, ind_ref, low_ref, high_ref, table_ref):
    sources = tab_ref.shape[0] // 8
    half = sources // 2
    size_x, size_y, _ = near_ref.shape
    value = [tab_ref[pl.ds(q, sources, stride=8), :] for q in range(5)]
    columns = []
    offset = value[3]
    for a in range(3):
        columns += parts_of(value[a], 2)
        offset = offset - value[a] * origin_ref[a]
    columns += parts_of(offset, 3) + parts_of(value[4], 2)
    put_table(table_ref, columns, half)
    mid_x, mid_y, mid_z = 0.5 * size_x, 0.5 * size_y, 0.5 * LANE
    sub = lax.broadcasted_iota(I32, (8, LANE), 0).astype(F32)
    at_z = lax.broadcasted_iota(I32, (8, LANE), 1).astype(F32) + (0.5 - mid_z)
    tiles = size_y // 8

    @pl.loop(0, size_x * tiles, unroll=8)
    def _(step):
        x = lax.shift_right_logical(step, tiles.bit_length() - 1)
        y = pl.multiple_of((step & (tiles - 1)) * 8, 8)
        index = near_ref[x, pl.ds(y, 8), :]
        found = look_up(table_ref, (2, 2, 2, 3, 2), half, [index[s:s + 1] for s in range(8)])
        at_x = x.astype(F32) + (0.5 - mid_x)
        at_y = sub + (y.astype(F32) + (0.5 - mid_y))
        distance = found[0] * at_x + found[1] * at_y + found[2] * at_z - found[3]
        indicator = 0.5 * (1.0 + jnp.tanh(distance / smear_width))
        ind_ref[x, pl.ds(y, 8), :] = indicator

        @pl.when(x < WIDE)
        def _():
            low_ref[0, x, pl.ds(y, 8), :] = indicator
            low_ref[1, x, pl.ds(y, 8), :] = found[4]

        @pl.when(x >= WIDE)
        def _():
            high_ref[0, x - WIDE, pl.ds(y, 8), :] = indicator
            high_ref[1, x - WIDE, pl.ds(y, 8), :] = found[4]


def cell_fields(tab, near, origin):
    sources = tab.shape[0] // 8
    out = jax.ShapeDtypeStruct(near.shape, F32)
    side = jax.ShapeDtypeStruct((2, WIDE) + near.shape[1:], F32)
    return pl.pallas_call(
        cell_kernel,
        name="cell_fields",
        out_shape=(out, side, side),
        in_specs=[VMEM, VMEM, pl.BlockSpec(memory_space=pltpu.SMEM)],
        out_specs=(VMEM, VMEM, VMEM),
        scratch_shapes=[pltpu.VMEM((11 * sources // 2, 2 * LANE), BF16)],
        compiler_params=pltpu.CompilerParams(vmem_limit_bytes=40 << 20),
        cost_estimate=pl.CostEstimate(flops=6 << 40, bytes_accessed=1 << 20, transcendentals=0),
    )(tab, near, origin)


def sample_vertices(field_ref, cell_ref, out_ref, table_ref):
    comps, size_x, size_y, _ = field_ref.shape
    half = size_x * size_y // 2
    for c in range(comps):
        for x in range(size_x):
            lanes = slice(LANE * (x // (size_x // 2)), LANE * (x // (size_x // 2)) + LANE)
            for p, part in enumerate(parts_of(field_ref[c, x], 2)):
                start = (2 * c + p) * half + (x % (size_x // 2)) * size_y
                table_ref[start:start + size_y, lanes] = part
    sources = cell_ref.shape[1] // LANE

    @pl.loop(0, sources // 8, unroll=8)
    def _(tile):
        for v in range(3):
            lines = [
                cell_ref[v:v + 1, pl.ds(pl.multiple_of((tile * 8 + s) * LANE, LANE), LANE)] for s in range(8)
            ]
            found = look_up(table_ref, (2, 2, 2), half, lines)
            for c in range(3):
                out_ref[pl.ds(tile * 72 + 3 * c + v, 8, stride=9), :] = found[c]


def home_kernel(back_ref, send_ref, out_ref, left_ref, right_ref, total_ref, sum_ref):
    dests = send_ref.shape[0]
    blocks = out_ref.shape[1] // (2 * LANE)
    chunk = right_ref.shape[1] // LANE
    total_ref[...] = jnp.zeros_like(total_ref)

    @pl.loop(0, dests // chunk)
    def _(step):
        for line in range(chunk):
            d = step * chunk + line
            index = send_ref[pl.ds(d, 1), :]
            at = slice(line * LANE, (line + 1) * LANE)
            right_ref[:, at] = one_hot(2 * LANE, index & (2 * LANE - 1))
            mine = one_hot(blocks, index >> 8)
            for r in range(9):
                value = jnp.broadcast_to(back_ref[pl.ds(d * 9 + r, 1), :], (blocks, LANE))
                head = value.astype(BF16)
                tail = (value - head.astype(F32)).astype(BF16)
                left_ref[r * blocks:(r + 1) * blocks, at] = mine * head
                left_ref[(9 + r) * blocks:(10 + r) * blocks, at] = mine * tail
        total_ref[...] += lax.dot_general(
            left_ref[...], right_ref[...], (((1,), (1,)), ((), ())), preferred_element_type=F32
        )

    rows = 9 * blocks
    for side in range(2):
        lanes = slice(side * LANE, (side + 1) * LANE)
        sum_ref[side * rows:(side + 1) * rows, :] = total_ref[0:rows, lanes] + total_ref[rows:2 * rows, lanes]
    for b in range(blocks):
        for side in range(2):
            at = (2 * b + side) * LANE
            out_ref[:, at:at + LANE] = sum_ref[pl.ds(side * rows + b, 9, stride=blocks), :]


def bring_home(back, send, triangles):
    blocks = triangles // (2 * LANE)
    chunk = 16
    return pl.pallas_call(
        home_kernel,
        name="bring_home",
        out_shape=jax.ShapeDtypeStruct((9, triangles), F32),
        in_specs=[VMEM, VMEM],
        out_specs=VMEM,
        scratch_shapes=[
            pltpu.VMEM((18 * blocks, chunk * LANE), BF16),
            pltpu.VMEM((2 * LANE, chunk * LANE), BF16),
            pltpu.VMEM((18 * blocks, 2 * LANE), F32),
            pltpu.VMEM((18 * blocks, LANE), F32),
        ],
        compiler_params=pltpu.CompilerParams(vmem_limit_bytes=40 << 20),
        cost_estimate=pl.CostEstimate(flops=2 << 40, bytes_accessed=1 << 20, transcendentals=0),
    )(back, send)


def pack_y_kernel(low_ref, high_ref, below_ref, above_ref, down_ref, up_ref):
    size_y = low_ref.shape[2]
    at = 0
    for c in range(low_ref.shape[0]):
        for ref in (below_ref, low_ref, high_ref, above_ref):
            for x in range(WIDE):
                down_ref[at:at + WIDE, :] = ref[c, x, 0:WIDE, :]
                up_ref[at:at + WIDE, :] = ref[c, x, size_y - WIDE:size_y, :]
                at += WIDE


def pack_y(low, high, below, above):
    out = jax.ShapeDtypeStruct((low.shape[0] * 4 * WIDE * WIDE, LANE), F32)
    return pl.pallas_call(
        pack_y_kernel,
        name="pack_y",
        out_shape=(out, out),
        in_specs=[VMEM] * 4,
        out_specs=(VMEM, VMEM),
        compiler_params=pltpu.CompilerParams(vmem_limit_bytes=16 << 20),
        cost_estimate=pl.CostEstimate(flops=1 << 20, bytes_accessed=1 << 20, transcendentals=0),
    )(low, high, below, above)


def pack_z_kernel(*refs):
    wide_ref, down_ref, up_ref = refs[-3:]
    lane = lax.broadcasted_iota(I32, (1, LANE), 1)
    group = lax.shift_right_logical(lane, 2)
    size_y = refs[0].shape[2]
    field = 0
    down = up = None
    for low_ref, high_ref, below_ref, above_ref, under_ref, over_ref in (refs[0:6], refs[6:12]):
        at = 0
        for c in range(low_ref.shape[0]):
            side = field % 2
            if side == 0:
                down = jnp.zeros((size_y + 2 * WIDE, LANE), F32)
                up = jnp.zeros((size_y + 2 * WIDE, LANE), F32)
            x = 0
            for ref in (below_ref, low_ref, high_ref, above_ref):
                for k in range(WIDE):
                    wide_ref[field, x, 0:WIDE] = under_ref[at:at + WIDE, :]
                    wide_ref[field, x, WIDE:WIDE + size_y] = ref[c, k]
                    wide_ref[field, x, WIDE + size_y:] = over_ref[at:at + WIDE, :]
                    plane = wide_ref[field, x]
                    slot = x + 4 * WIDE * side
                    here = group == slot
                    shift = WIDE * slot
                    moved = pltpu.roll(plane, shift, 1) if shift else plane
                    down = jnp.where(here, moved, down)
                    shift = (shift + WIDE) % LANE
                    moved = pltpu.roll(plane, shift, 1) if shift else plane
                    up = jnp.where(here, moved, up)
                    at += WIDE
                    x += 1
            rows = pl.ds((field // 2) * (size_y + 2 * WIDE), size_y + 2 * WIDE)
            down_ref[rows, :] = down
            up_ref[rows, :] = up
            field += 1


def pack_z(first, second):
    fields = first[0].shape[0] + second[0].shape[0]
    rows = first[0].shape[2] + 2 * WIDE
    message = jax.ShapeDtypeStruct(((fields + 1) // 2 * rows, LANE), F32)
    return pl.pallas_call(
        pack_z_kernel,
        name="pack_z",
        out_shape=(jax.ShapeDtypeStruct((fields, 4 * WIDE, rows, LANE), F32), message, message),
        in_specs=[VMEM] * 12,
        out_specs=(VMEM,) * 3,
        compiler_params=pltpu.CompilerParams(vmem_limit_bytes=24 << 20),
        cost_estimate=pl.CostEstimate(flops=1 << 20, bytes_accessed=1 << 20, transcendentals=0),
    )(*first, *second)


SPARE = 8


def sweep_kernel(wide_ref, before_ref, after_ref, cell_ref, out_ref, sample_ref, one_ref, two_ref, coef_ref, table_ref):
    planes, rows = wide_ref.shape[1:3]
    size_y = rows - 2 * WIDE
    stride = rows + 2 * SPARE

    def ends(count):
        lane = lax.broadcasted_iota(I32, (count, LANE), 1)
        return lane == 0, lane == LANE - 1

    lane = lax.broadcasted_iota(I32, (rows, LANE), 1)
    for field in range(5):
        pair = slice((field // 2) * rows, (field // 2 + 1) * rows)
        after, before = after_ref[pair, :], before_ref[pair, :]
        for x in range(planes):
            shift = WIDE * (x + planes * (field % 2))
            near = pltpu.roll(after, (LANE - shift) % LANE, 1) if shift else after
            far = pltpu.roll(before, LANE - WIDE - shift, 1) if LANE - WIDE - shift else before
            edge = jnp.where(lane < WIDE, near, jnp.where(lane >= LANE - WIDE, far, 0.0))
            one_ref[field, x, SPARE:SPARE + rows] = wide_ref[field, x]
            one_ref[field, x, stride + SPARE:stride + SPARE + rows] = edge

    def neighbours(middle, edge):
        first, last = ends(middle.shape[0])
        return (
            pltpu.roll(jnp.where(first, edge, middle), LANE - 1, 1),
            pltpu.roll(jnp.where(last, edge, middle), 1, 1),
        )

    @pl.loop(1, planes - 1, unroll=2)
    def _(x):
        for at in (SPARE, stride + SPARE):
            other = SPARE if at > SPARE else stride + SPARE
            here = pl.ds(at, rows)
            centre = one_ref[3, x, here]
            later, sooner = neighbours(centre, one_ref[3, x, pl.ds(other, rows)])
            density = rho_liquid + (rho_gas - rho_liquid) * centre
            viscosity = mu_liquid + (mu_gas - mu_liquid) * centre
            scale = time_step / density
            pull = one_ref[4, x, here] * scale * 0.5
            coef_ref[0, x, here] = viscosity * scale
            coef_ref[1, x, here] = pull * (one_ref[3, x + 1, here] - one_ref[3, x - 1, here])
            coef_ref[2, x, here] = pull * (one_ref[3, x, pl.ds(at + 1, rows)] - one_ref[3, x, pl.ds(at - 1, rows)])
            coef_ref[3, x, here] = pull * (later - sooner)

    def sweep(source, margin, offset, count, store):
        starts = (offset, stride + offset) if margin else (offset,)

        @pl.loop(WIDE - margin, planes - WIDE + margin, unroll=2)
        def _(x):
            for c in range(3):
                planes_here = [source[c, x, pl.ds(stride * k + offset, count)] for k in range(2)]
                for k, at in enumerate(starts):
                    here = pl.ds(at, count)
                    centre = planes_here[k]
                    later, sooner = neighbours(centre, planes_here[1 - k])
                    laplace = source[c, x + 1, here] + source[c, x - 1, here]
                    laplace = laplace + source[c, x, pl.ds(at + 1, count)] + source[c, x, pl.ds(at - 1, count)]
                    laplace = laplace + later + sooner - 6.0 * centre
                    store(c, x, here, centre + (coef_ref[0, x, here] * laplace + coef_ref[1 + c, x, here]))

    def into(ref):
        def store(c, x, here, value):
            ref[c, x, here] = value
        return store

    def into_result(c, x, here, value):
        out_ref[c, x - WIDE] = value

    sweep(one_ref, 3, SPARE, rows, into(two_ref))
    sweep(two_ref, 2, SPARE, rows, into(one_ref))
    sweep(one_ref, 1, SPARE, rows, into(two_ref))
    sweep(two_ref, 0, SPARE + WIDE, size_y, into_result)
    sample_vertices(out_ref, cell_ref, sample_ref, table_ref)


def swept(wide, before, after, cells):
    _, planes, rows, _ = wide.shape
    size_x, size_y = planes - 2 * WIDE, rows - 2 * WIDE
    sources = cells.shape[1] // LANE
    stride = rows + 2 * SPARE
    return pl.pallas_call(
        sweep_kernel,
        name="sweeps",
        out_shape=(
            jax.ShapeDtypeStruct((3, size_x, size_y, LANE), F32),
            jax.ShapeDtypeStruct((sources * 9, LANE), F32),
        ),
        in_specs=[VMEM] * 4,
        out_specs=(VMEM, VMEM),
        scratch_shapes=[
            pltpu.VMEM((5, planes, 2 * stride, LANE), F32),
            pltpu.VMEM((3, planes, 2 * stride, LANE), F32),
            pltpu.VMEM((4, planes, 2 * stride, LANE), F32),
            pltpu.VMEM((6 * size_x * size_y // 2, 2 * LANE), BF16),
        ],
        compiler_params=pltpu.CompilerParams(vmem_limit_bytes=40 << 20),
        cost_estimate=pl.CostEstimate(flops=10 << 40, bytes_accessed=1 << 20, transcendentals=0),
    )(wide, before, after, cells)


def both_ways(down, up, axis):
    count = lax.axis_size(axis)
    above = lax.ppermute(down, axis, [((i + 1) % count, i) for i in range(count)])
    below = lax.ppermute(up, axis, [(i, (i + 1) % count) for i in range(count)])
    return below, above


def per_device(tri_geom, send_index, near_index, return_cell, velocity):
    size_x, size_y, size_z = near_index.shape
    group_x, group_y = lax.axis_size("gx"), lax.axis_size("gy")
    vel_low, vel_high = velocity[:, :WIDE], velocity[:, WIDE:]
    vel_below, vel_above = both_ways(vel_low, vel_high, "gx")
    mid_z = (lax.axis_index("gz") * size_z + size_z // 2).astype(F32)
    mid_x, mid_y = 0.5 * group_x * size_x, 0.5 * group_y * size_y
    outgoing = send_tables(tri_geom, send_index, jnp.stack([jnp.float32(mid_x), jnp.float32(mid_y), mid_z]))
    arrived = lax.all_to_all(
        outgoing.reshape(-1, 8, LANE), ("gx", "gy"), split_axis=0, concat_axis=0, tiled=True
    ).reshape(-1, LANE)
    vel_down, vel_up = pack_y(vel_low, vel_high, vel_below, vel_above)
    vel_under, vel_over = both_ways(vel_down, vel_up, "gy")
    arrived, vel_under, vel_over = lax.optimization_barrier((arrived, vel_under, vel_over))
    own_x = (lax.axis_index("gx") * size_x + size_x // 2).astype(F32) - mid_x
    own_y = (lax.axis_index("gy") * size_y + size_y // 2).astype(F32) - mid_y
    indicator, low, high = cell_fields(arrived, near_index, jnp.stack([own_x, own_y, jnp.float32(0.0)]))
    below, above = both_ways(low, high, "gx")
    down, up = pack_y(low, high, below, above)
    under, over = both_ways(down, up, "gy")
    wide, down, up = pack_z(
        (vel_low, vel_high, vel_below, vel_above, vel_under, vel_over), (low, high, below, above, under, over)
    )
    before, after = both_ways(down, up, "gz")
    current, samples = swept(wide, before, after, return_cell)
    returned = lax.all_to_all(
        samples.reshape(-1, 9 * LANE), ("gx", "gy"), split_axis=0, concat_axis=0, tiled=True
    ).reshape(-1, LANE)
    return (current, indicator, bring_home(returned, send_index, tri_geom.shape[1]))


def solution(mesh):
    placed = (
        P(None, ("gx", "gy", "gz")),
        P(("gx", "gy", "gz"), None),
        P("gx", "gy", "gz"),
        P(None, ("gx", "gy", "gz")),
        P(None, "gx", "gy", "gz"),
    )
    return jax.shard_map(
        per_device,
        mesh=mesh,
        in_specs=placed,
        out_specs=(P(None, "gx", "gy", "gz"), P("gx", "gy", "gz"), P(None, ("gx", "gy", "gz"))),
        check_vma=False,
    )
```

```python
import jax
import jax.numpy as jnp
from jax import lax
from jax.experimental import pallas as pl
from jax.experimental.pallas import tpu as pltpu
from jax.sharding import PartitionSpec as P

NSWEEP = 4
WIDE = NSWEEP

time_step = 0.04
smear_width = 4.0
rho_liquid = 1.0
rho_gas = 0.05
mu_liquid = 2.0
mu_gas = 0.2

F32, BF16, I32 = jnp.float32, jnp.bfloat16, jnp.int32
LANE = 128
SPAN = 2
VMEM = pl.BlockSpec(memory_space=pltpu.VMEM)


def one_hot(rows, index):
    level = lax.broadcasted_iota(I32, (rows, index.shape[1]), 0).astype(F32).astype(BF16)
    same = level == index.astype(F32).astype(BF16)
    return jnp.where(same, jnp.ones_like(level), jnp.zeros_like(level))


def fold_lines(lines):
    sub = lax.broadcasted_iota(I32, (8, LANE), 0)
    step = 1
    while step < 8:
        low = (sub & step) == 0
        lines = [
            jnp.where(low, even, odd) + pltpu.roll(jnp.where(low, odd, even), step, 0)
            for even, odd in zip(lines[0::2], lines[1::2])
        ]
        step *= 2
    return lines[0]


def parts_of(value, count):
    out = []
    for _ in range(count - 1):
        head = value.astype(BF16)
        out.append(head)
        value = value - head.astype(F32)
    out.append(value.astype(BF16))
    return out


def put_table(table_ref, columns, halves):
    for q, column in enumerate(columns):
        table_ref[q * halves:(q + 1) * halves, 0:LANE] = column[0:halves]
        table_ref[q * halves:(q + 1) * halves, LANE:2 * LANE] = column[halves:2 * halves]


def look_up(table_ref, groups, half, lines):
    shift = half.bit_length() - 1
    tiles = half // 8
    sub = lax.broadcasted_iota(I32, (8, LANE), 0)
    count = sum(groups)
    found = [[] for _ in groups]
    for pair in range(8 // SPAN):
        index = jnp.concatenate(lines[SPAN * pair:SPAN * (pair + 1)], axis=1)
        row = index >> 7
        hot = one_hot(2 * LANE, ((row >> shift) << 7) + (index & 127))
        product = jnp.dot(table_ref[...], hot, preferred_element_type=F32)
        place = jnp.where(index < 0, -1, row & (half - 1))
        for side in range(SPAN):
            here = place[:, side * LANE:(side + 1) * LANE]
            masks = [sub + 8 * t == here for t in range(tiles)]
            picked = []
            for q in range(count):
                total = jnp.zeros((8, LANE), F32)
                for t in range(tiles):
                    start = q * half + 8 * t
                    total = jnp.where(masks[t], product[start:start + 8, side * LANE:(side + 1) * LANE], total)
                picked.append(total)
            at = 0
            for g, size in enumerate(groups):
                total = picked[at]
                for other in picked[at + 1:at + size]:
                    total = total + other
                found[g].append(total)
                at += size
    return [fold_lines(column) for column in found]


def send_kernel(geom_ref, send_ref, origin_ref, out_ref, dense_ref, table_ref):
    rows = geom_ref.shape[1] // LANE
    half = rows // 2
    for h in range(rows):
        dense_ref[pl.ds(h, 10, stride=rows), :] = geom_ref[:, h * LANE:(h + 1) * LANE]
    geom = [dense_ref[r * rows:(r + 1) * rows, :] for r in range(10)]
    one = [geom[3 + a] - geom[a] for a in range(3)]
    two = [geom[6 + a] - geom[a] for a in range(3)]
    normal = [
        one[1] * two[2] - one[2] * two[1],
        one[2] * two[0] - one[0] * two[2],
        one[0] * two[1] - one[1] * two[0],
    ]
    length = jnp.sqrt(normal[0] * normal[0] + normal[1] * normal[1] + normal[2] * normal[2])
    scale = jnp.maximum(length, 1.0)
    columns = []
    offset = jnp.zeros_like(length)
    for a in range(3):
        head, tail = parts_of(normal[a] / scale, 2)
        columns += [head, tail]
        centre = (geom[a] + geom[3 + a] + geom[6 + a]) / 3.0 - origin_ref[a]
        offset = offset + (head.astype(F32) + tail.astype(F32)) * centre
    columns += parts_of(offset, 3) + parts_of(geom[9], 2)
    put_table(table_ref, columns, half)

    @pl.loop(0, send_ref.shape[0] // 8, unroll=8)
    def _(tile):
        index = send_ref[pl.ds(tile * 8, 8), :]
        found = look_up(table_ref, (2, 2, 2, 3, 2), half, [index[s:s + 1] for s in range(8)])
        for q, value in enumerate(found):
            out_ref[pl.ds(tile * 64 + q, 8, stride=8), :] = value


def send_tables(geom, send, origin):
    rows = geom.shape[1] // LANE
    dests = send.shape[0]
    return pl.pallas_call(
        send_kernel,
        name="send_tables",
        out_shape=jax.ShapeDtypeStruct((dests * 8, LANE), F32),
        in_specs=[VMEM, VMEM, pl.BlockSpec(memory_space=pltpu.SMEM)],
        out_specs=VMEM,
        scratch_shapes=[pltpu.VMEM((10 * rows, LANE), F32), pltpu.VMEM((11 * rows // 2, 2 * LANE), BF16)],
        compiler_params=pltpu.CompilerParams(vmem_limit_bytes=40 << 20),
        cost_estimate=pl.CostEstimate(flops=2 << 40, bytes_accessed=1 << 20, transcendentals=0),
    )(geom, send, origin)


def cell_kernel(tab_ref, near_ref, origin_ref, ind_ref, low_ref, high_ref, table_ref):
    sources = tab_ref.shape[0] // 8
    half = sources // 2
    size_x, size_y, _ = near_ref.shape
    value = [tab_ref[pl.ds(q, sources, stride=8), :] for q in range(5)]
    columns = []
    offset = value[3]
    for a in range(3):
        columns += parts_of(value[a], 2)
        offset = offset - value[a] * origin_ref[a]
    columns += parts_of(offset, 3) + parts_of(value[4], 2)
    put_table(table_ref, columns, half)
    mid_x, mid_y, mid_z = 0.5 * size_x, 0.5 * size_y, 0.5 * LANE
    sub = lax.broadcasted_iota(I32, (8, LANE), 0).astype(F32)
    at_z = lax.broadcasted_iota(I32, (8, LANE), 1).astype(F32) + (0.5 - mid_z)
    tiles = size_y // 8

    for side_ref, start in ((low_ref, 0), (high_ref, WIDE)):

        @pl.loop(0, WIDE * tiles, unroll=8)
        def _(step):
            x = lax.shift_right_logical(step, tiles.bit_length() - 1)
            y = pl.multiple_of((step & (tiles - 1)) * 8, 8)
            index = near_ref[start + x, pl.ds(y, 8), :]
            found = look_up(table_ref, (2, 2, 2, 3, 2), half, [index[s:s + 1] for s in range(8)])
            at_x = x.astype(F32) + (start + 0.5 - mid_x)
            at_y = sub + (y.astype(F32) + (0.5 - mid_y))
            distance = found[0] * at_x + found[1] * at_y + found[2] * at_z - found[3]
            indicator = 0.5 * (1.0 + jnp.tanh(distance / smear_width))
            ind_ref[start + x, pl.ds(y, 8), :] = indicator
            side_ref[0, x, pl.ds(y, 8), :] = indicator
            side_ref[1, x, pl.ds(y, 8), :] = found[4]


def cell_fields(tab, near, origin):
    sources = tab.shape[0] // 8
    out = jax.ShapeDtypeStruct(near.shape, F32)
    side = jax.ShapeDtypeStruct((2, WIDE) + near.shape[1:], F32)
    return pl.pallas_call(
        cell_kernel,
        name="cell_fields",
        out_shape=(out, side, side),
        in_specs=[VMEM, VMEM, pl.BlockSpec(memory_space=pltpu.SMEM)],
        out_specs=(VMEM, VMEM, VMEM),
        scratch_shapes=[pltpu.VMEM((11 * sources // 2, 2 * LANE), BF16)],
        compiler_params=pltpu.CompilerParams(vmem_limit_bytes=40 << 20),
        cost_estimate=pl.CostEstimate(flops=6 << 40, bytes_accessed=1 << 20, transcendentals=0),
    )(tab, near, origin)


def sample_vertices(field_ref, cell_ref, out_ref, table_ref):
    comps, size_x, size_y, _ = field_ref.shape
    half = size_x * size_y // 2
    for c in range(comps):
        for x in range(size_x):
            lanes = slice(LANE * (x // (size_x // 2)), LANE * (x // (size_x // 2)) + LANE)
            for p, part in enumerate(parts_of(field_ref[c, x], 2)):
                start = (2 * c + p) * half + (x % (size_x // 2)) * size_y
                table_ref[start:start + size_y, lanes] = part
    sources = cell_ref.shape[1] // LANE

    @pl.loop(0, sources // 8, unroll=8)
    def _(tile):
        for v in range(3):
            lines = [
                cell_ref[v:v + 1, pl.ds(pl.multiple_of((tile * 8 + s) * LANE, LANE), LANE)] for s in range(8)
            ]
            found = look_up(table_ref, (2, 2, 2), half, lines)
            for c in range(3):
                out_ref[pl.ds(tile * 72 + 3 * c + v, 8, stride=9), :] = found[c]


def home_kernel(back_ref, send_ref, out_ref, left_ref, right_ref, total_ref, sum_ref):
    dests = send_ref.shape[0]
    blocks = out_ref.shape[1] // (2 * LANE)
    chunk = right_ref.shape[1] // LANE
    total_ref[...] = jnp.zeros_like(total_ref)

    @pl.loop(0, dests // chunk)
    def _(step):
        for line in range(chunk):
            d = step * chunk + line
            index = send_ref[pl.ds(d, 1), :]
            at = slice(line * LANE, (line + 1) * LANE)
            right_ref[:, at] = one_hot(2 * LANE, index & (2 * LANE - 1))
            mine = one_hot(blocks, index >> 8)
            for r in range(9):
                value = jnp.broadcast_to(back_ref[pl.ds(d * 9 + r, 1), :], (blocks, LANE))
                head = value.astype(BF16)
                tail = (value - head.astype(F32)).astype(BF16)
                left_ref[r * blocks:(r + 1) * blocks, at] = mine * head
                left_ref[(9 + r) * blocks:(10 + r) * blocks, at] = mine * tail
        total_ref[...] += lax.dot_general(
            left_ref[...], right_ref[...], (((1,), (1,)), ((), ())), preferred_element_type=F32
        )

    rows = 9 * blocks
    for side in range(2):
        lanes = slice(side * LANE, (side + 1) * LANE)
        sum_ref[side * rows:(side + 1) * rows, :] = total_ref[0:rows, lanes] + total_ref[rows:2 * rows, lanes]
    for b in range(blocks):
        for side in range(2):
            at = (2 * b + side) * LANE
            out_ref[:, at:at + LANE] = sum_ref[pl.ds(side * rows + b, 9, stride=blocks), :]


def bring_home(back, send, triangles):
    blocks = triangles // (2 * LANE)
    chunk = 16
    return pl.pallas_call(
        home_kernel,
        name="bring_home",
        out_shape=jax.ShapeDtypeStruct((9, triangles), F32),
        in_specs=[VMEM, VMEM],
        out_specs=VMEM,
        scratch_shapes=[
            pltpu.VMEM((18 * blocks, chunk * LANE), BF16),
            pltpu.VMEM((2 * LANE, chunk * LANE), BF16),
            pltpu.VMEM((18 * blocks, 2 * LANE), F32),
            pltpu.VMEM((18 * blocks, LANE), F32),
        ],
        compiler_params=pltpu.CompilerParams(vmem_limit_bytes=40 << 20),
        cost_estimate=pl.CostEstimate(flops=2 << 40, bytes_accessed=1 << 20, transcendentals=0),
    )(back, send)


def pack_y_kernel(low_ref, high_ref, below_ref, above_ref, down_ref, up_ref):
    size_y = low_ref.shape[2]
    at = 0
    for c in range(low_ref.shape[0]):
        for ref in (below_ref, low_ref, high_ref, above_ref):
            for x in range(WIDE):
                down_ref[at:at + WIDE, :] = ref[c, x, 0:WIDE, :]
                up_ref[at:at + WIDE, :] = ref[c, x, size_y - WIDE:size_y, :]
                at += WIDE


def pack_y(low, high, below, above):
    out = jax.ShapeDtypeStruct((low.shape[0] * 4 * WIDE * WIDE, LANE), F32)
    return pl.pallas_call(
        pack_y_kernel,
        name="pack_y",
        out_shape=(out, out),
        in_specs=[VMEM] * 4,
        out_specs=(VMEM, VMEM),
        compiler_params=pltpu.CompilerParams(vmem_limit_bytes=16 << 20),
        cost_estimate=pl.CostEstimate(flops=1 << 20, bytes_accessed=1 << 20, transcendentals=0),
    )(low, high, below, above)


def pack_z_kernel(*refs):
    wide_ref, down_ref, up_ref = refs[-3:]
    lane = lax.broadcasted_iota(I32, (1, LANE), 1)
    group = lax.shift_right_logical(lane, 2)
    size_y = refs[0].shape[2]
    field = 0
    down = up = None
    for low_ref, high_ref, below_ref, above_ref, under_ref, over_ref in (refs[0:6], refs[6:12]):
        at = 0
        for c in range(low_ref.shape[0]):
            side = field % 2
            if side == 0:
                down = jnp.zeros((size_y + 2 * WIDE, LANE), F32)
                up = jnp.zeros((size_y + 2 * WIDE, LANE), F32)
            x = 0
            for ref in (below_ref, low_ref, high_ref, above_ref):
                for k in range(WIDE):
                    wide_ref[field, x, 0:WIDE] = under_ref[at:at + WIDE, :]
                    wide_ref[field, x, WIDE:WIDE + size_y] = ref[c, k]
                    wide_ref[field, x, WIDE + size_y:] = over_ref[at:at + WIDE, :]
                    plane = wide_ref[field, x]
                    slot = x + 4 * WIDE * side
                    here = group == slot
                    shift = WIDE * slot
                    moved = pltpu.roll(plane, shift, 1) if shift else plane
                    down = jnp.where(here, moved, down)
                    shift = (shift + WIDE) % LANE
                    moved = pltpu.roll(plane, shift, 1) if shift else plane
                    up = jnp.where(here, moved, up)
                    at += WIDE
                    x += 1
            rows = pl.ds((field // 2) * (size_y + 2 * WIDE), size_y + 2 * WIDE)
            down_ref[rows, :] = down
            up_ref[rows, :] = up
            field += 1


def pack_z(first, second):
    fields = first[0].shape[0] + second[0].shape[0]
    rows = first[0].shape[2] + 2 * WIDE
    message = jax.ShapeDtypeStruct(((fields + 1) // 2 * rows, LANE), F32)
    return pl.pallas_call(
        pack_z_kernel,
        name="pack_z",
        out_shape=(jax.ShapeDtypeStruct((fields, 4 * WIDE, rows, LANE), F32), message, message),
        in_specs=[VMEM] * 12,
        out_specs=(VMEM,) * 3,
        compiler_params=pltpu.CompilerParams(vmem_limit_bytes=24 << 20),
        cost_estimate=pl.CostEstimate(flops=1 << 20, bytes_accessed=1 << 20, transcendentals=0),
    )(*first, *second)


SPARE = 8


def sweep_kernel(wide_ref, before_ref, after_ref, cell_ref, out_ref, sample_ref, one_ref, two_ref, coef_ref, table_ref):
    planes, rows = wide_ref.shape[1:3]
    size_y = rows - 2 * WIDE
    stride = rows + 2 * SPARE

    def ends(count):
        lane = lax.broadcasted_iota(I32, (count, LANE), 1)
        return lane == 0, lane == LANE - 1

    lane = lax.broadcasted_iota(I32, (rows, LANE), 1)
    for field in range(5):
        pair = slice((field // 2) * rows, (field // 2 + 1) * rows)
        after, before = after_ref[pair, :], before_ref[pair, :]
        for x in range(planes):
            shift = WIDE * (x + planes * (field % 2))
            near = pltpu.roll(after, (LANE - shift) % LANE, 1) if shift else after
            far = pltpu.roll(before, LANE - WIDE - shift, 1) if LANE - WIDE - shift else before
            edge = jnp.where(lane < WIDE, near, jnp.where(lane >= LANE - WIDE, far, 0.0))
            one_ref[field, x, SPARE:SPARE + rows] = wide_ref[field, x]
            one_ref[field, x, stride + SPARE:stride + SPARE + rows] = edge

    def neighbours(middle, edge):
        first, last = ends(middle.shape[0])
        return (
            pltpu.roll(jnp.where(first, edge, middle), LANE - 1, 1),
            pltpu.roll(jnp.where(last, edge, middle), 1, 1),
        )

    @pl.loop(1, planes - 1, unroll=2)
    def _(x):
        for at in (SPARE, stride + SPARE):
            other = SPARE if at > SPARE else stride + SPARE
            here = pl.ds(at, rows)
            centre = one_ref[3, x, here]
            later, sooner = neighbours(centre, one_ref[3, x, pl.ds(other, rows)])
            density = rho_liquid + (rho_gas - rho_liquid) * centre
            viscosity = mu_liquid + (mu_gas - mu_liquid) * centre
            scale = time_step / density
            pull = one_ref[4, x, here] * scale * 0.5
            coef_ref[0, x, here] = viscosity * scale
            coef_ref[1, x, here] = pull * (one_ref[3, x + 1, here] - one_ref[3, x - 1, here])
            coef_ref[2, x, here] = pull * (one_ref[3, x, pl.ds(at + 1, rows)] - one_ref[3, x, pl.ds(at - 1, rows)])
            coef_ref[3, x, here] = pull * (later - sooner)

    def sweep(source, margin, offset, count, store):
        starts = (offset, stride + offset) if margin else (offset,)

        @pl.loop(WIDE - margin, planes - WIDE + margin, unroll=2)
        def _(x):
            for c in range(3):
                planes_here = [source[c, x, pl.ds(stride * k + offset, count)] for k in range(2)]
                for k, at in enumerate(starts):
                    here = pl.ds(at, count)
                    centre = planes_here[k]
                    later, sooner = neighbours(centre, planes_here[1 - k])
                    laplace = source[c, x + 1, here] + source[c, x - 1, here]
                    laplace = laplace + source[c, x, pl.ds(at + 1, count)] + source[c, x, pl.ds(at - 1, count)]
                    laplace = laplace + later + sooner - 6.0 * centre
                    store(c, x, here, centre + (coef_ref[0, x, here] * laplace + coef_ref[1 + c, x, here]))

    def into(ref):
        def store(c, x, here, value):
            ref[c, x, here] = value
        return store

    def into_result(c, x, here, value):
        out_ref[c, x - WIDE] = value

    sweep(one_ref, 3, SPARE, rows, into(two_ref))
    sweep(two_ref, 2, SPARE, rows, into(one_ref))
    sweep(one_ref, 1, SPARE, rows, into(two_ref))
    sweep(two_ref, 0, SPARE + WIDE, size_y, into_result)
    sample_vertices(out_ref, cell_ref, sample_ref, table_ref)


def swept(wide, before, after, cells):
    _, planes, rows, _ = wide.shape
    size_x, size_y = planes - 2 * WIDE, rows - 2 * WIDE
    sources = cells.shape[1] // LANE
    stride = rows + 2 * SPARE
    return pl.pallas_call(
        sweep_kernel,
        name="sweeps",
        out_shape=(
            jax.ShapeDtypeStruct((3, size_x, size_y, LANE), F32),
            jax.ShapeDtypeStruct((sources * 9, LANE), F32),
        ),
        in_specs=[VMEM] * 4,
        out_specs=(VMEM, VMEM),
        scratch_shapes=[
            pltpu.VMEM((5, planes, 2 * stride, LANE), F32),
            pltpu.VMEM((3, planes, 2 * stride, LANE), F32),
            pltpu.VMEM((4, planes, 2 * stride, LANE), F32),
            pltpu.VMEM((6 * size_x * size_y // 2, 2 * LANE), BF16),
        ],
        compiler_params=pltpu.CompilerParams(vmem_limit_bytes=40 << 20),
        cost_estimate=pl.CostEstimate(flops=10 << 40, bytes_accessed=1 << 20, transcendentals=0),
    )(wide, before, after, cells)


def both_ways(down, up, axis):
    count = lax.axis_size(axis)
    above = lax.ppermute(down, axis, [((i + 1) % count, i) for i in range(count)])
    below = lax.ppermute(up, axis, [(i, (i + 1) % count) for i in range(count)])
    return below, above


def per_device(tri_geom, send_index, near_index, return_cell, velocity):
    size_x, size_y, size_z = near_index.shape
    group_x, group_y = lax.axis_size("gx"), lax.axis_size("gy")
    vel_low, vel_high = velocity[:, :WIDE], velocity[:, WIDE:]
    vel_below, vel_above = both_ways(vel_low, vel_high, "gx")
    mid_z = (lax.axis_index("gz") * size_z + size_z // 2).astype(F32)
    mid_x, mid_y = 0.5 * group_x * size_x, 0.5 * group_y * size_y
    outgoing = send_tables(tri_geom, send_index, jnp.stack([jnp.float32(mid_x), jnp.float32(mid_y), mid_z]))
    arrived = lax.all_to_all(
        outgoing.reshape(-1, 8, LANE), ("gx", "gy"), split_axis=0, concat_axis=0, tiled=True
    ).reshape(-1, LANE)
    vel_down, vel_up = pack_y(vel_low, vel_high, vel_below, vel_above)
    vel_under, vel_over = both_ways(vel_down, vel_up, "gy")
    own_x = (lax.axis_index("gx") * size_x + size_x // 2).astype(F32) - mid_x
    own_y = (lax.axis_index("gy") * size_y + size_y // 2).astype(F32) - mid_y
    indicator, low, high = cell_fields(arrived, near_index, jnp.stack([own_x, own_y, jnp.float32(0.0)]))
    below, above = both_ways(low, high, "gx")
    down, up = pack_y(low, high, below, above)
    under, over = both_ways(down, up, "gy")
    wide, down, up = pack_z(
        (vel_low, vel_high, vel_below, vel_above, vel_under, vel_over), (low, high, below, above, under, over)
    )
    before, after = both_ways(down, up, "gz")
    current, samples = swept(wide, before, after, return_cell)
    returned = lax.all_to_all(
        samples.reshape(-1, 9 * LANE), ("gx", "gy"), split_axis=0, concat_axis=0, tiled=True
    ).reshape(-1, LANE)
    return (current, indicator, bring_home(returned, send_index, tri_geom.shape[1]))


def solution(mesh):
    placed = (
        P(None, ("gx", "gy", "gz")),
        P(("gx", "gy", "gz"), None),
        P("gx", "gy", "gz"),
        P(None, ("gx", "gy", "gz")),
        P(None, "gx", "gy", "gz"),
    )
    return jax.shard_map(
        per_device,
        mesh=mesh,
        in_specs=placed,
        out_specs=(P(None, "gx", "gy", "gz"), P("gx", "gy", "gz"), P(None, ("gx", "gy", "gz"))),
        check_vma=False,
    )
```

```python
import jax
import jax.numpy as jnp
from jax import lax
from jax.experimental import pallas as pl
from jax.experimental.pallas import tpu as pltpu
from jax.sharding import PartitionSpec as P

NSWEEP = 4
WIDE = NSWEEP

time_step = 0.04
smear_width = 4.0
rho_liquid = 1.0
rho_gas = 0.05
mu_liquid = 2.0
mu_gas = 0.2

F32, BF16, I32 = jnp.float32, jnp.bfloat16, jnp.int32
LANE = 128
SPAN = 2
VMEM = pl.BlockSpec(memory_space=pltpu.VMEM)


def one_hot(rows, index):
    level = lax.broadcasted_iota(I32, (rows, index.shape[1]), 0).astype(F32).astype(BF16)
    same = level == index.astype(F32).astype(BF16)
    return jnp.where(same, jnp.ones_like(level), jnp.zeros_like(level))


def fold_lines(lines):
    sub = lax.broadcasted_iota(I32, (8, LANE), 0)
    step = 1
    while step < 8:
        low = (sub & step) == 0
        lines = [
            jnp.where(low, even, odd) + pltpu.roll(jnp.where(low, odd, even), step, 0)
            for even, odd in zip(lines[0::2], lines[1::2])
        ]
        step *= 2
    return lines[0]


def parts_of(value, count):
    out = []
    for _ in range(count - 1):
        head = value.astype(BF16)
        out.append(head)
        value = value - head.astype(F32)
    out.append(value.astype(BF16))
    return out


def put_table(table_ref, columns, halves):
    for q, column in enumerate(columns):
        table_ref[q * halves:(q + 1) * halves, 0:LANE] = column[0:halves]
        table_ref[q * halves:(q + 1) * halves, LANE:2 * LANE] = column[halves:2 * halves]


def look_up(table_ref, groups, half, lines):
    shift = half.bit_length() - 1
    tiles = half // 8
    sub = lax.broadcasted_iota(I32, (8, LANE), 0)
    count = sum(groups)
    found = [[] for _ in groups]
    for pair in range(8 // SPAN):
        index = jnp.concatenate(lines[SPAN * pair:SPAN * (pair + 1)], axis=1)
        row = index >> 7
        hot = one_hot(2 * LANE, ((row >> shift) << 7) + (index & 127))
        product = jnp.dot(table_ref[...], hot, preferred_element_type=F32)
        place = jnp.where(index < 0, -1, row & (half - 1))
        for side in range(SPAN):
            here = place[:, side * LANE:(side + 1) * LANE]
            masks = [sub + 8 * t == here for t in range(tiles)]
            picked = []
            for q in range(count):
                total = jnp.zeros((8, LANE), F32)
                for t in range(tiles):
                    start = q * half + 8 * t
                    total = jnp.where(masks[t], product[start:start + 8, side * LANE:(side + 1) * LANE], total)
                picked.append(total)
            at = 0
            for g, size in enumerate(groups):
                total = picked[at]
                for other in picked[at + 1:at + size]:
                    total = total + other
                found[g].append(total)
                at += size
    return [fold_lines(column) for column in found]


def send_kernel(geom_ref, send_ref, origin_ref, out_ref, dense_ref, table_ref):
    rows = geom_ref.shape[1] // LANE
    half = rows // 2
    for h in range(rows):
        dense_ref[pl.ds(h, 10, stride=rows), :] = geom_ref[:, h * LANE:(h + 1) * LANE]
    geom = [dense_ref[r * rows:(r + 1) * rows, :] for r in range(10)]
    one = [geom[3 + a] - geom[a] for a in range(3)]
    two = [geom[6 + a] - geom[a] for a in range(3)]
    normal = [
        one[1] * two[2] - one[2] * two[1],
        one[2] * two[0] - one[0] * two[2],
        one[0] * two[1] - one[1] * two[0],
    ]
    length = jnp.sqrt(normal[0] * normal[0] + normal[1] * normal[1] + normal[2] * normal[2])
    scale = jnp.maximum(length, 1.0)
    columns = []
    offset = jnp.zeros_like(length)
    for a in range(3):
        head, tail = parts_of(normal[a] / scale, 2)
        columns += [head, tail]
        centre = (geom[a] + geom[3 + a] + geom[6 + a]) / 3.0 - origin_ref[a]
        offset = offset + (head.astype(F32) + tail.astype(F32)) * centre
    columns += parts_of(offset, 3) + parts_of(geom[9], 2)
    put_table(table_ref, columns, half)

    @pl.loop(0, send_ref.shape[0] // 8, unroll=8)
    def _(tile):
        index = send_ref[pl.ds(tile * 8, 8), :]
        found = look_up(table_ref, (2, 2, 2, 3, 2), half, [index[s:s + 1] for s in range(8)])
        for q, value in enumerate(found):
            out_ref[pl.ds(tile * 40 + q, 8, stride=5), :] = value


def send_tables(geom, send, origin):
    rows = geom.shape[1] // LANE
    dests = send.shape[0]
    return pl.pallas_call(
        send_kernel,
        name="send_tables",
        out_shape=jax.ShapeDtypeStruct((dests * 5, LANE), F32),
        in_specs=[VMEM, VMEM, pl.BlockSpec(memory_space=pltpu.SMEM)],
        out_specs=VMEM,
        scratch_shapes=[pltpu.VMEM((10 * rows, LANE), F32), pltpu.VMEM((11 * rows // 2, 2 * LANE), BF16)],
        compiler_params=pltpu.CompilerParams(vmem_limit_bytes=40 << 20),
        cost_estimate=pl.CostEstimate(flops=2 << 40, bytes_accessed=1 << 20, transcendentals=0),
    )(geom, send, origin)


def cell_kernel(tab_ref, near_ref, origin_ref, ind_ref, low_ref, high_ref, table_ref):
    sources = tab_ref.shape[0] // 5
    half = sources // 2
    size_x, size_y, _ = near_ref.shape
    value = [tab_ref[pl.ds(q, sources, stride=5), :] for q in range(5)]
    columns = []
    offset = value[3]
    for a in range(3):
        columns += parts_of(value[a], 2)
        offset = offset - value[a] * origin_ref[a]
    columns += parts_of(offset, 3) + parts_of(value[4], 2)
    put_table(table_ref, columns, half)
    mid_x, mid_y, mid_z = 0.5 * size_x, 0.5 * size_y, 0.5 * LANE
    sub = lax.broadcasted_iota(I32, (8, LANE), 0).astype(F32)
    at_z = lax.broadcasted_iota(I32, (8, LANE), 1).astype(F32) + (0.5 - mid_z)
    tiles = size_y // 8

    for side_ref, start in ((low_ref, 0), (high_ref, WIDE)):

        @pl.loop(0, WIDE * tiles, unroll=8)
        def _(step):
            x = lax.shift_right_logical(step, tiles.bit_length() - 1)
            y = pl.multiple_of((step & (tiles - 1)) * 8, 8)
            index = near_ref[start + x, pl.ds(y, 8), :]
            found = look_up(table_ref, (2, 2, 2, 3, 2), half, [index[s:s + 1] for s in range(8)])
            at_x = x.astype(F32) + (start + 0.5 - mid_x)
            at_y = sub + (y.astype(F32) + (0.5 - mid_y))
            distance = found[0] * at_x + found[1] * at_y + found[2] * at_z - found[3]
            indicator = 0.5 * (1.0 + jnp.tanh(distance / smear_width))
            ind_ref[start + x, pl.ds(y, 8), :] = indicator
            side_ref[0, x, pl.ds(y, 8), :] = indicator
            side_ref[1, x, pl.ds(y, 8), :] = found[4]


def cell_fields(tab, near, origin):
    sources = tab.shape[0] // 5
    out = jax.ShapeDtypeStruct(near.shape, F32)
    side = jax.ShapeDtypeStruct((2, WIDE) + near.shape[1:], F32)
    return pl.pallas_call(
        cell_kernel,
        name="cell_fields",
        out_shape=(out, side, side),
        in_specs=[VMEM, VMEM, pl.BlockSpec(memory_space=pltpu.SMEM)],
        out_specs=(VMEM, VMEM, VMEM),
        scratch_shapes=[pltpu.VMEM((11 * sources // 2, 2 * LANE), BF16)],
        compiler_params=pltpu.CompilerParams(vmem_limit_bytes=40 << 20),
        cost_estimate=pl.CostEstimate(flops=6 << 40, bytes_accessed=1 << 20, transcendentals=0),
    )(tab, near, origin)


def sample_vertices(field_ref, cell_ref, out_ref, table_ref):
    comps, size_x, size_y, _ = field_ref.shape
    half = size_x * size_y // 2
    for c in range(comps):
        for x in range(size_x):
            lanes = slice(LANE * (x // (size_x // 2)), LANE * (x // (size_x // 2)) + LANE)
            for p, part in enumerate(parts_of(field_ref[c, x], 2)):
                start = (2 * c + p) * half + (x % (size_x // 2)) * size_y
                table_ref[start:start + size_y, lanes] = part
    sources = cell_ref.shape[1] // LANE

    @pl.loop(0, sources // 8, unroll=8)
    def _(tile):
        for v in range(3):
            lines = [
                cell_ref[v:v + 1, pl.ds(pl.multiple_of((tile * 8 + s) * LANE, LANE), LANE)] for s in range(8)
            ]
            found = look_up(table_ref, (2, 2, 2), half, lines)
            for c in range(3):
                out_ref[pl.ds(tile * 72 + 3 * c + v, 8, stride=9), :] = found[c]


def home_kernel(back_ref, send_ref, out_ref, left_ref, right_ref, total_ref, sum_ref):
    dests = send_ref.shape[0]
    blocks = out_ref.shape[1] // (2 * LANE)
    chunk = right_ref.shape[1] // LANE
    total_ref[...] = jnp.zeros_like(total_ref)

    @pl.loop(0, dests // chunk)
    def _(step):
        for line in range(chunk):
            d = step * chunk + line
            index = send_ref[pl.ds(d, 1), :]
            at = slice(line * LANE, (line + 1) * LANE)
            right_ref[:, at] = one_hot(2 * LANE, index & (2 * LANE - 1))
            mine = one_hot(blocks, index >> 8)
            for r in range(9):
                value = jnp.broadcast_to(back_ref[pl.ds(d * 9 + r, 1), :], (blocks, LANE))
                head = value.astype(BF16)
                tail = (value - head.astype(F32)).astype(BF16)
                left_ref[r * blocks:(r + 1) * blocks, at] = mine * head
                left_ref[(9 + r) * blocks:(10 + r) * blocks, at] = mine * tail
        total_ref[...] += lax.dot_general(
            left_ref[...], right_ref[...], (((1,), (1,)), ((), ())), preferred_element_type=F32
        )

    rows = 9 * blocks
    for side in range(2):
        lanes = slice(side * LANE, (side + 1) * LANE)
        sum_ref[side * rows:(side + 1) * rows, :] = total_ref[0:rows, lanes] + total_ref[rows:2 * rows, lanes]
    for b in range(blocks):
        for side in range(2):
            at = (2 * b + side) * LANE
            out_ref[:, at:at + LANE] = sum_ref[pl.ds(side * rows + b, 9, stride=blocks), :]


def bring_home(back, send, triangles):
    blocks = triangles // (2 * LANE)
    chunk = 16
    return pl.pallas_call(
        home_kernel,
        name="bring_home",
        out_shape=jax.ShapeDtypeStruct((9, triangles), F32),
        in_specs=[VMEM, VMEM],
        out_specs=VMEM,
        scratch_shapes=[
            pltpu.VMEM((18 * blocks, chunk * LANE), BF16),
            pltpu.VMEM((2 * LANE, chunk * LANE), BF16),
            pltpu.VMEM((18 * blocks, 2 * LANE), F32),
            pltpu.VMEM((18 * blocks, LANE), F32),
        ],
        compiler_params=pltpu.CompilerParams(vmem_limit_bytes=40 << 20),
        cost_estimate=pl.CostEstimate(flops=2 << 40, bytes_accessed=1 << 20, transcendentals=0),
    )(back, send)


def pack_y_kernel(low_ref, high_ref, below_ref, above_ref, down_ref, up_ref):
    size_y = low_ref.shape[2]
    at = 0
    for c in range(low_ref.shape[0]):
        for ref in (below_ref, low_ref, high_ref, above_ref):
            for x in range(WIDE):
                down_ref[at:at + WIDE, :] = ref[c, x, 0:WIDE, :]
                up_ref[at:at + WIDE, :] = ref[c, x, size_y - WIDE:size_y, :]
                at += WIDE


def pack_y(low, high, below, above):
    out = jax.ShapeDtypeStruct((low.shape[0] * 4 * WIDE * WIDE, LANE), F32)
    return pl.pallas_call(
        pack_y_kernel,
        name="pack_y",
        out_shape=(out, out),
        in_specs=[VMEM] * 4,
        out_specs=(VMEM, VMEM),
        compiler_params=pltpu.CompilerParams(vmem_limit_bytes=16 << 20),
        cost_estimate=pl.CostEstimate(flops=1 << 20, bytes_accessed=1 << 20, transcendentals=0),
    )(low, high, below, above)


def pack_z_kernel(*refs):
    wide_ref, down_ref, up_ref = refs[-3:]
    lane = lax.broadcasted_iota(I32, (1, LANE), 1)
    group = lax.shift_right_logical(lane, 2)
    size_y = refs[0].shape[2]
    field = 0
    down = up = None
    for low_ref, high_ref, below_ref, above_ref, under_ref, over_ref in (refs[0:6], refs[6:12]):
        at = 0
        for c in range(low_ref.shape[0]):
            side = field % 2
            if side == 0:
                down = jnp.zeros((size_y + 2 * WIDE, LANE), F32)
                up = jnp.zeros((size_y + 2 * WIDE, LANE), F32)
            x = 0
            for ref in (below_ref, low_ref, high_ref, above_ref):
                for k in range(WIDE):
                    wide_ref[field, x, 0:WIDE] = under_ref[at:at + WIDE, :]
                    wide_ref[field, x, WIDE:WIDE + size_y] = ref[c, k]
                    wide_ref[field, x, WIDE + size_y:] = over_ref[at:at + WIDE, :]
                    plane = wide_ref[field, x]
                    slot = x + 4 * WIDE * side
                    here = group == slot
                    shift = WIDE * slot
                    moved = pltpu.roll(plane, shift, 1) if shift else plane
                    down = jnp.where(here, moved, down)
                    shift = (shift + WIDE) % LANE
                    moved = pltpu.roll(plane, shift, 1) if shift else plane
                    up = jnp.where(here, moved, up)
                    at += WIDE
                    x += 1
            rows = pl.ds((field // 2) * (size_y + 2 * WIDE), size_y + 2 * WIDE)
            down_ref[rows, :] = down
            up_ref[rows, :] = up
            field += 1


def pack_z(first, second):
    fields = first[0].shape[0] + second[0].shape[0]
    rows = first[0].shape[2] + 2 * WIDE
    message = jax.ShapeDtypeStruct(((fields + 1) // 2 * rows, LANE), F32)
    return pl.pallas_call(
        pack_z_kernel,
        name="pack_z",
        out_shape=(jax.ShapeDtypeStruct((fields, 4 * WIDE, rows, LANE), F32), message, message),
        in_specs=[VMEM] * 12,
        out_specs=(VMEM,) * 3,
        compiler_params=pltpu.CompilerParams(vmem_limit_bytes=24 << 20),
        cost_estimate=pl.CostEstimate(flops=1 << 20, bytes_accessed=1 << 20, transcendentals=0),
    )(*first, *second)


SPARE = 8


def sweep_kernel(wide_ref, before_ref, after_ref, cell_ref, out_ref, sample_ref, one_ref, two_ref, coef_ref, table_ref):
    planes, rows = wide_ref.shape[1:3]
    size_y = rows - 2 * WIDE
    stride = rows + 2 * SPARE

    def ends(count):
        lane = lax.broadcasted_iota(I32, (count, LANE), 1)
        return lane == 0, lane == LANE - 1

    lane = lax.broadcasted_iota(I32, (rows, LANE), 1)
    for field in range(5):
        pair = slice((field // 2) * rows, (field // 2 + 1) * rows)
        after, before = after_ref[pair, :], before_ref[pair, :]
        for x in range(planes):
            shift = WIDE * (x + planes * (field % 2))
            near = pltpu.roll(after, (LANE - shift) % LANE, 1) if shift else after
            far = pltpu.roll(before, LANE - WIDE - shift, 1) if LANE - WIDE - shift else before
            edge = jnp.where(lane < WIDE, near, jnp.where(lane >= LANE - WIDE, far, 0.0))
            one_ref[field, x, SPARE:SPARE + rows] = wide_ref[field, x]
            one_ref[field, x, stride + SPARE:stride + SPARE + rows] = edge

    def neighbours(middle, edge):
        first, last = ends(middle.shape[0])
        return (
            pltpu.roll(jnp.where(first, edge, middle), LANE - 1, 1),
            pltpu.roll(jnp.where(last, edge, middle), 1, 1),
        )

    @pl.loop(1, planes - 1, unroll=2)
    def _(x):
        for at in (SPARE, stride + SPARE):
            other = SPARE if at > SPARE else stride + SPARE
            here = pl.ds(at, rows)
            centre = one_ref[3, x, here]
            later, sooner = neighbours(centre, one_ref[3, x, pl.ds(other, rows)])
            density = rho_liquid + (rho_gas - rho_liquid) * centre
            viscosity = mu_liquid + (mu_gas - mu_liquid) * centre
            scale = time_step / density
            pull = one_ref[4, x, here] * scale * 0.5
            coef_ref[0, x, here] = viscosity * scale
            coef_ref[1, x, here] = pull * (one_ref[3, x + 1, here] - one_ref[3, x - 1, here])
            coef_ref[2, x, here] = pull * (one_ref[3, x, pl.ds(at + 1, rows)] - one_ref[3, x, pl.ds(at - 1, rows)])
            coef_ref[3, x, here] = pull * (later - sooner)

    def sweep(source, margin, offset, count, store):
        starts = (offset, stride + offset) if margin else (offset,)

        @pl.loop(WIDE - margin, planes - WIDE + margin, unroll=2)
        def _(x):
            for c in range(3):
                planes_here = [source[c, x, pl.ds(stride * k + offset, count)] for k in range(2)]
                for k, at in enumerate(starts):
                    here = pl.ds(at, count)
                    centre = planes_here[k]
                    later, sooner = neighbours(centre, planes_here[1 - k])
                    laplace = source[c, x + 1, here] + source[c, x - 1, here]
                    laplace = laplace + source[c, x, pl.ds(at + 1, count)] + source[c, x, pl.ds(at - 1, count)]
                    laplace = laplace + later + sooner - 6.0 * centre
                    store(c, x, here, centre + (coef_ref[0, x, here] * laplace + coef_ref[1 + c, x, here]))

    def into(ref):
        def store(c, x, here, value):
            ref[c, x, here] = value
        return store

    def into_result(c, x, here, value):
        out_ref[c, x - WIDE] = value

    sweep(one_ref, 3, SPARE, rows, into(two_ref))
    sweep(two_ref, 2, SPARE, rows, into(one_ref))
    sweep(one_ref, 1, SPARE, rows, into(two_ref))
    sweep(two_ref, 0, SPARE + WIDE, size_y, into_result)
    sample_vertices(out_ref, cell_ref, sample_ref, table_ref)


def swept(wide, before, after, cells):
    _, planes, rows, _ = wide.shape
    size_x, size_y = planes - 2 * WIDE, rows - 2 * WIDE
    sources = cells.shape[1] // LANE
    stride = rows + 2 * SPARE
    return pl.pallas_call(
        sweep_kernel,
        name="sweeps",
        out_shape=(
            jax.ShapeDtypeStruct((3, size_x, size_y, LANE), F32),
            jax.ShapeDtypeStruct((sources * 9, LANE), F32),
        ),
        in_specs=[VMEM] * 4,
        out_specs=(VMEM, VMEM),
        scratch_shapes=[
            pltpu.VMEM((5, planes, 2 * stride, LANE), F32),
            pltpu.VMEM((3, planes, 2 * stride, LANE), F32),
            pltpu.VMEM((4, planes, 2 * stride, LANE), F32),
            pltpu.VMEM((6 * size_x * size_y // 2, 2 * LANE), BF16),
        ],
        compiler_params=pltpu.CompilerParams(vmem_limit_bytes=40 << 20),
        cost_estimate=pl.CostEstimate(flops=10 << 40, bytes_accessed=1 << 20, transcendentals=0),
    )(wide, before, after, cells)


def both_ways(down, up, axis):
    count = lax.axis_size(axis)
    above = lax.ppermute(down, axis, [((i + 1) % count, i) for i in range(count)])
    below = lax.ppermute(up, axis, [(i, (i + 1) % count) for i in range(count)])
    return below, above


def per_device(tri_geom, send_index, near_index, return_cell, velocity):
    size_x, size_y, size_z = near_index.shape
    group_x, group_y = lax.axis_size("gx"), lax.axis_size("gy")
    vel_low, vel_high = velocity[:, :WIDE], velocity[:, WIDE:]
    vel_below, vel_above = both_ways(vel_low, vel_high, "gx")
    mid_z = (lax.axis_index("gz") * size_z + size_z // 2).astype(F32)
    mid_x, mid_y = 0.5 * group_x * size_x, 0.5 * group_y * size_y
    outgoing = send_tables(tri_geom, send_index, jnp.stack([jnp.float32(mid_x), jnp.float32(mid_y), mid_z]))
    arrived = lax.all_to_all(
        outgoing.reshape(-1, 5 * LANE), ("gx", "gy"), split_axis=0, concat_axis=0, tiled=True
    ).reshape(-1, LANE)
    vel_down, vel_up = pack_y(vel_low, vel_high, vel_below, vel_above)
    vel_under, vel_over = both_ways(vel_down, vel_up, "gy")
    own_x = (lax.axis_index("gx") * size_x + size_x // 2).astype(F32) - mid_x
    own_y = (lax.axis_index("gy") * size_y + size_y // 2).astype(F32) - mid_y
    indicator, low, high = cell_fields(arrived, near_index, jnp.stack([own_x, own_y, jnp.float32(0.0)]))
    below, above = both_ways(low, high, "gx")
    down, up = pack_y(low, high, below, above)
    under, over = both_ways(down, up, "gy")
    wide, down, up = pack_z(
        (vel_low, vel_high, vel_below, vel_above, vel_under, vel_over), (low, high, below, above, under, over)
    )
    before, after = both_ways(down, up, "gz")
    current, samples = swept(wide, before, after, return_cell)
    returned = lax.all_to_all(
        samples.reshape(-1, 9 * LANE), ("gx", "gy"), split_axis=0, concat_axis=0, tiled=True
    ).reshape(-1, LANE)
    return (current, indicator, bring_home(returned, send_index, tri_geom.shape[1]))


def solution(mesh):
    placed = (
        P(None, ("gx", "gy", "gz")),
        P(("gx", "gy", "gz"), None),
        P("gx", "gy", "gz"),
        P(None, ("gx", "gy", "gz")),
        P(None, "gx", "gy", "gz"),
    )
    return jax.shard_map(
        per_device,
        mesh=mesh,
        in_specs=placed,
        out_specs=(P(None, "gx", "gy", "gz"), P("gx", "gy", "gz"), P(None, ("gx", "gy", "gz"))),
        check_vma=False,
    )
```

```python
import jax
import jax.numpy as jnp
from jax import lax
from jax.experimental import pallas as pl
from jax.experimental.pallas import tpu as pltpu
from jax.sharding import PartitionSpec as P

NSWEEP = 4
WIDE = NSWEEP

time_step = 0.04
smear_width = 4.0
rho_liquid = 1.0
rho_gas = 0.05
mu_liquid = 2.0
mu_gas = 0.2

F32, BF16, I32 = jnp.float32, jnp.bfloat16, jnp.int32
LANE = 128
SPAN = 2
VMEM = pl.BlockSpec(memory_space=pltpu.VMEM)


def one_hot(rows, index):
    level = lax.broadcasted_iota(I32, (rows, index.shape[1]), 0).astype(F32).astype(BF16)
    same = level == index.astype(F32).astype(BF16)
    return jnp.where(same, jnp.ones_like(level), jnp.zeros_like(level))


def fold_lines(lines):
    sub = lax.broadcasted_iota(I32, (8, LANE), 0)
    step = 1
    while step < 8:
        low = (sub & step) == 0
        lines = [
            jnp.where(low, even, odd) + pltpu.roll(jnp.where(low, odd, even), step, 0)
            for even, odd in zip(lines[0::2], lines[1::2])
        ]
        step *= 2
    return lines[0]


def parts_of(value, count):
    out = []
    for _ in range(count - 1):
        head = value.astype(BF16)
        out.append(head)
        value = value - head.astype(F32)
    out.append(value.astype(BF16))
    return out


def put_table(table_ref, columns, halves):
    for q, column in enumerate(columns):
        table_ref[q * halves:(q + 1) * halves, 0:LANE] = column[0:halves]
        table_ref[q * halves:(q + 1) * halves, LANE:2 * LANE] = column[halves:2 * halves]


def look_up(table_ref, groups, half, lines):
    shift = half.bit_length() - 1
    tiles = half // 8
    sub = lax.broadcasted_iota(I32, (8, LANE), 0)
    count = sum(groups)
    found = [[] for _ in groups]
    for pair in range(8 // SPAN):
        index = jnp.concatenate(lines[SPAN * pair:SPAN * (pair + 1)], axis=1)
        row = index >> 7
        hot = one_hot(2 * LANE, ((row >> shift) << 7) + (index & 127))
        product = jnp.dot(table_ref[...], hot, preferred_element_type=F32)
        place = jnp.where(index < 0, -1, row & (half - 1))
        for side in range(SPAN):
            here = place[:, side * LANE:(side + 1) * LANE]
            masks = [sub + 8 * t == here for t in range(tiles)]
            picked = []
            for q in range(count):
                total = jnp.zeros((8, LANE), F32)
                for t in range(tiles):
                    start = q * half + 8 * t
                    total = jnp.where(masks[t], product[start:start + 8, side * LANE:(side + 1) * LANE], total)
                picked.append(total)
            at = 0
            for g, size in enumerate(groups):
                total = picked[at]
                for other in picked[at + 1:at + size]:
                    total = total + other
                found[g].append(total)
                at += size
    return [fold_lines(column) for column in found]


def send_kernel(geom_ref, send_ref, origin_ref, out_ref, dense_ref, table_ref):
    rows = geom_ref.shape[1] // LANE
    half = rows // 2
    for h in range(rows):
        dense_ref[pl.ds(h, 10, stride=rows), :] = geom_ref[:, h * LANE:(h + 1) * LANE]
    geom = [dense_ref[r * rows:(r + 1) * rows, :] for r in range(10)]
    one = [geom[3 + a] - geom[a] for a in range(3)]
    two = [geom[6 + a] - geom[a] for a in range(3)]
    normal = [
        one[1] * two[2] - one[2] * two[1],
        one[2] * two[0] - one[0] * two[2],
        one[0] * two[1] - one[1] * two[0],
    ]
    length = jnp.sqrt(normal[0] * normal[0] + normal[1] * normal[1] + normal[2] * normal[2])
    scale = jnp.maximum(length, 1.0)
    columns = []
    offset = jnp.zeros_like(length)
    for a in range(3):
        head, tail = parts_of(normal[a] / scale, 2)
        columns += [head, tail]
        centre = (geom[a] + geom[3 + a] + geom[6 + a]) / 3.0 - origin_ref[a]
        offset = offset + (head.astype(F32) + tail.astype(F32)) * centre
    columns += parts_of(offset, 3) + parts_of(geom[9], 2)
    put_table(table_ref, columns, half)

    @pl.loop(0, send_ref.shape[0] // 8, unroll=8)
    def _(tile):
        index = send_ref[pl.ds(tile * 8, 8), :]
        found = look_up(table_ref, (2, 2, 2, 3, 2), half, [index[s:s + 1] for s in range(8)])
        for q, value in enumerate(found):
            out_ref[pl.ds(tile * 40 + q, 8, stride=5), :] = value


def send_tables(geom, send, origin):
    rows = geom.shape[1] // LANE
    dests = send.shape[0]
    return pl.pallas_call(
        send_kernel,
        name="send_tables",
        out_shape=jax.ShapeDtypeStruct((dests * 5, LANE), F32),
        in_specs=[VMEM, VMEM, pl.BlockSpec(memory_space=pltpu.SMEM)],
        out_specs=VMEM,
        scratch_shapes=[pltpu.VMEM((10 * rows, LANE), F32), pltpu.VMEM((11 * rows // 2, 2 * LANE), BF16)],
        compiler_params=pltpu.CompilerParams(vmem_limit_bytes=40 << 20),
        cost_estimate=pl.CostEstimate(flops=2 << 40, bytes_accessed=1 << 20, transcendentals=0),
    )(geom, send, origin)


def cell_kernel(tab_ref, near_ref, origin_ref, ind_ref, low_ref, high_ref, table_ref):
    sources = tab_ref.shape[0] // 5
    half = sources // 2
    size_x, size_y, _ = near_ref.shape
    value = [tab_ref[pl.ds(q, sources, stride=5), :] for q in range(5)]
    columns = []
    offset = value[3]
    for a in range(3):
        columns += parts_of(value[a], 2)
        offset = offset - value[a] * origin_ref[a]
    columns += parts_of(offset, 3) + parts_of(value[4], 2)
    put_table(table_ref, columns, half)
    mid_x, mid_y, mid_z = 0.5 * size_x, 0.5 * size_y, 0.5 * LANE
    sub = lax.broadcasted_iota(I32, (8, LANE), 0).astype(F32)
    at_z = lax.broadcasted_iota(I32, (8, LANE), 1).astype(F32) + (0.5 - mid_z)
    tiles = size_y // 8

    for side_ref, start in ((low_ref, 0), (high_ref, WIDE)):

        @pl.loop(0, WIDE * tiles, unroll=8)
        def _(step):
            x = lax.shift_right_logical(step, tiles.bit_length() - 1)
            y = pl.multiple_of((step & (tiles - 1)) * 8, 8)
            index = near_ref[start + x, pl.ds(y, 8), :]
            found = look_up(table_ref, (2, 2, 2, 3, 2), half, [index[s:s + 1] for s in range(8)])
            at_x = x.astype(F32) + (start + 0.5 - mid_x)
            at_y = sub + (y.astype(F32) + (0.5 - mid_y))
            distance = found[0] * at_x + found[1] * at_y + found[2] * at_z - found[3]
            indicator = 0.5 * (1.0 + jnp.tanh(distance / smear_width))
            ind_ref[start + x, pl.ds(y, 8), :] = indicator
            side_ref[0, x, pl.ds(y, 8), :] = indicator
            side_ref[1, x, pl.ds(y, 8), :] = found[4]


def cell_fields(tab, near, origin):
    sources = tab.shape[0] // 5
    out = jax.ShapeDtypeStruct(near.shape, F32)
    side = jax.ShapeDtypeStruct((2, WIDE) + near.shape[1:], F32)
    return pl.pallas_call(
        cell_kernel,
        name="cell_fields",
        out_shape=(out, side, side),
        in_specs=[VMEM, VMEM, pl.BlockSpec(memory_space=pltpu.SMEM)],
        out_specs=(VMEM, VMEM, VMEM),
        scratch_shapes=[pltpu.VMEM((11 * sources // 2, 2 * LANE), BF16)],
        compiler_params=pltpu.CompilerParams(vmem_limit_bytes=40 << 20),
        cost_estimate=pl.CostEstimate(flops=6 << 40, bytes_accessed=1 << 20, transcendentals=0),
    )(tab, near, origin)


def sample_vertices(field_ref, cell_ref, out_ref, table_ref):
    comps, size_x, size_y, _ = field_ref.shape
    half = size_x * size_y // 2
    for c in range(comps):
        for x in range(size_x):
            lanes = slice(LANE * (x // (size_x // 2)), LANE * (x // (size_x // 2)) + LANE)
            for p, part in enumerate(parts_of(field_ref[c, x], 2)):
                start = (2 * c + p) * half + (x % (size_x // 2)) * size_y
                table_ref[start:start + size_y, lanes] = part
    sources = cell_ref.shape[1] // LANE

    @pl.loop(0, sources // 8, unroll=8)
    def _(tile):
        for v in range(3):
            lines = [
                cell_ref[v:v + 1, pl.ds(pl.multiple_of((tile * 8 + s) * LANE, LANE), LANE)] for s in range(8)
            ]
            found = look_up(table_ref, (2, 2, 2), half, lines)
            for c in range(3):
                out_ref[pl.ds(tile * 72 + 3 * c + v, 8, stride=9), :] = found[c]


def home_kernel(back_ref, send_ref, out_ref, left_ref, right_ref, total_ref, sum_ref):
    dests = send_ref.shape[0]
    blocks = out_ref.shape[1] // (2 * LANE)
    chunk = right_ref.shape[1] // LANE
    total_ref[...] = jnp.zeros_like(total_ref)

    @pl.loop(0, dests // chunk)
    def _(step):
        for line in range(chunk):
            d = step * chunk + line
            index = send_ref[pl.ds(d, 1), :]
            at = slice(line * LANE, (line + 1) * LANE)
            right_ref[:, at] = one_hot(2 * LANE, index & (2 * LANE - 1))
            mine = one_hot(blocks, index >> 8)
            for r in range(9):
                value = jnp.broadcast_to(back_ref[pl.ds(d * 9 + r, 1), :], (blocks, LANE))
                head = value.astype(BF16)
                tail = (value - head.astype(F32)).astype(BF16)
                left_ref[r * blocks:(r + 1) * blocks, at] = mine * head
                left_ref[(9 + r) * blocks:(10 + r) * blocks, at] = mine * tail
        total_ref[...] += lax.dot_general(
            left_ref[...], right_ref[...], (((1,), (1,)), ((), ())), preferred_element_type=F32
        )

    rows = 9 * blocks
    for side in range(2):
        lanes = slice(side * LANE, (side + 1) * LANE)
        sum_ref[side * rows:(side + 1) * rows, :] = total_ref[0:rows, lanes] + total_ref[rows:2 * rows, lanes]
    for b in range(blocks):
        for side in range(2):
            at = (2 * b + side) * LANE
            out_ref[:, at:at + LANE] = sum_ref[pl.ds(side * rows + b, 9, stride=blocks), :]


def bring_home(back, send, triangles):
    blocks = triangles // (2 * LANE)
    chunk = 16
    return pl.pallas_call(
        home_kernel,
        name="bring_home",
        out_shape=jax.ShapeDtypeStruct((9, triangles), F32),
        in_specs=[VMEM, VMEM],
        out_specs=VMEM,
        scratch_shapes=[
            pltpu.VMEM((18 * blocks, chunk * LANE), BF16),
            pltpu.VMEM((2 * LANE, chunk * LANE), BF16),
            pltpu.VMEM((18 * blocks, 2 * LANE), F32),
            pltpu.VMEM((18 * blocks, LANE), F32),
        ],
        compiler_params=pltpu.CompilerParams(vmem_limit_bytes=40 << 20),
        cost_estimate=pl.CostEstimate(flops=2 << 40, bytes_accessed=1 << 20, transcendentals=0),
    )(back, send)


def pack_y_kernel(low_ref, high_ref, below_ref, above_ref, down_ref, up_ref):
    size_y = low_ref.shape[2]
    at = 0
    for c in range(low_ref.shape[0]):
        for ref in (below_ref, low_ref, high_ref, above_ref):
            for x in range(WIDE):
                down_ref[at:at + WIDE, :] = ref[c, x, 0:WIDE, :]
                up_ref[at:at + WIDE, :] = ref[c, x, size_y - WIDE:size_y, :]
                at += WIDE


def pack_y(low, high, below, above):
    out = jax.ShapeDtypeStruct((low.shape[0] * 4 * WIDE * WIDE, LANE), F32)
    return pl.pallas_call(
        pack_y_kernel,
        name="pack_y",
        out_shape=(out, out),
        in_specs=[VMEM] * 4,
        out_specs=(VMEM, VMEM),
        compiler_params=pltpu.CompilerParams(vmem_limit_bytes=16 << 20),
        cost_estimate=pl.CostEstimate(flops=1 << 20, bytes_accessed=1 << 20, transcendentals=0),
    )(low, high, below, above)


def pack_z_kernel(first, refs):
    low_ref, high_ref, below_ref, above_ref, under_ref, over_ref = refs[0:6]
    wide_ref, down_ref, up_ref = refs[-3:]
    lane = lax.broadcasted_iota(I32, (1, LANE), 1)
    group = lax.shift_right_logical(lane, 2)
    size_y = low_ref.shape[2]
    height = size_y + 2 * WIDE
    if len(refs) > 9:
        done = (first + 1) // 2 * height
        down_ref[0:done, :] = refs[6][...]
        up_ref[0:done, :] = refs[7][...]
    at = 0
    for c in range(low_ref.shape[0]):
        field = first + c
        side = field % 2
        rows = slice((field // 2) * height, (field // 2 + 1) * height)
        down = down_ref[rows, :] if side else jnp.zeros((height, LANE), F32)
        up = up_ref[rows, :] if side else jnp.zeros((height, LANE), F32)
        x = 0
        for ref in (below_ref, low_ref, high_ref, above_ref):
            for k in range(WIDE):
                wide_ref[c, x, 0:WIDE] = under_ref[at:at + WIDE, :]
                wide_ref[c, x, WIDE:WIDE + size_y] = ref[c, k]
                wide_ref[c, x, WIDE + size_y:] = over_ref[at:at + WIDE, :]
                plane = wide_ref[c, x]
                slot = x + 4 * WIDE * side
                here = group == slot
                shift = WIDE * slot
                moved = pltpu.roll(plane, shift, 1) if shift else plane
                down = jnp.where(here, moved, down)
                shift = (shift + WIDE) % LANE
                moved = pltpu.roll(plane, shift, 1) if shift else plane
                up = jnp.where(here, moved, up)
                at += WIDE
                x += 1
        down_ref[rows, :] = down
        up_ref[rows, :] = up


def pack_z(first, planes, begun=()):
    fields, _, size_y, _ = planes[0].shape
    height = size_y + 2 * WIDE
    message = jax.ShapeDtypeStruct(((first + fields + 1) // 2 * height, LANE), F32)
    return pl.pallas_call(
        lambda *refs: pack_z_kernel(first, refs),
        name="pack_z",
        out_shape=(jax.ShapeDtypeStruct((fields, 4 * WIDE, height, LANE), F32), message, message),
        in_specs=[VMEM] * (6 + len(begun)),
        out_specs=(VMEM,) * 3,
        compiler_params=pltpu.CompilerParams(vmem_limit_bytes=24 << 20),
        cost_estimate=pl.CostEstimate(flops=1 << 20, bytes_accessed=1 << 20, transcendentals=0),
    )(*planes, *begun)


SPARE = 8


def sweep_kernel(wide_ref, more_ref, before_ref, after_ref, cell_ref, out_ref, sample_ref, one_ref, two_ref, coef_ref, table_ref):
    planes, rows = wide_ref.shape[1:3]
    size_y = rows - 2 * WIDE
    stride = rows + 2 * SPARE

    def ends(count):
        lane = lax.broadcasted_iota(I32, (count, LANE), 1)
        return lane == 0, lane == LANE - 1

    lane = lax.broadcasted_iota(I32, (rows, LANE), 1)
    for field in range(5):
        pair = slice((field // 2) * rows, (field // 2 + 1) * rows)
        after, before = after_ref[pair, :], before_ref[pair, :]
        for x in range(planes):
            shift = WIDE * (x + planes * (field % 2))
            near = pltpu.roll(after, (LANE - shift) % LANE, 1) if shift else after
            far = pltpu.roll(before, LANE - WIDE - shift, 1) if LANE - WIDE - shift else before
            edge = jnp.where(lane < WIDE, near, jnp.where(lane >= LANE - WIDE, far, 0.0))
            one_ref[field, x, SPARE:SPARE + rows] = wide_ref[field, x] if field < 3 else more_ref[field - 3, x]
            one_ref[field, x, stride + SPARE:stride + SPARE + rows] = edge

    def neighbours(middle, edge):
        first, last = ends(middle.shape[0])
        return (
            pltpu.roll(jnp.where(first, edge, middle), LANE - 1, 1),
            pltpu.roll(jnp.where(last, edge, middle), 1, 1),
        )

    @pl.loop(1, planes - 1, unroll=2)
    def _(x):
        for at in (SPARE, stride + SPARE):
            other = SPARE if at > SPARE else stride + SPARE
            here = pl.ds(at, rows)
            centre = one_ref[3, x, here]
            later, sooner = neighbours(centre, one_ref[3, x, pl.ds(other, rows)])
            density = rho_liquid + (rho_gas - rho_liquid) * centre
            viscosity = mu_liquid + (mu_gas - mu_liquid) * centre
            scale = time_step / density
            pull = one_ref[4, x, here] * scale * 0.5
            coef_ref[0, x, here] = viscosity * scale
            coef_ref[1, x, here] = pull * (one_ref[3, x + 1, here] - one_ref[3, x - 1, here])
            coef_ref[2, x, here] = pull * (one_ref[3, x, pl.ds(at + 1, rows)] - one_ref[3, x, pl.ds(at - 1, rows)])
            coef_ref[3, x, here] = pull * (later - sooner)

    def sweep(source, margin, offset, count, store):
        starts = (offset, stride + offset) if margin else (offset,)

        @pl.loop(WIDE - margin, planes - WIDE + margin, unroll=2)
        def _(x):
            for c in range(3):
                planes_here = [source[c, x, pl.ds(stride * k + offset, count)] for k in range(2)]
                for k, at in enumerate(starts):
                    here = pl.ds(at, count)
                    centre = planes_here[k]
                    later, sooner = neighbours(centre, planes_here[1 - k])
                    laplace = source[c, x + 1, here] + source[c, x - 1, here]
                    laplace = laplace + source[c, x, pl.ds(at + 1, count)] + source[c, x, pl.ds(at - 1, count)]
                    laplace = laplace + later + sooner - 6.0 * centre
                    store(c, x, here, centre + (coef_ref[0, x, here] * laplace + coef_ref[1 + c, x, here]))

    def into(ref):
        def store(c, x, here, value):
            ref[c, x, here] = value
        return store

    def into_result(c, x, here, value):
        out_ref[c, x - WIDE] = value

    sweep(one_ref, 3, SPARE, rows, into(two_ref))
    sweep(two_ref, 2, SPARE, rows, into(one_ref))
    sweep(one_ref, 1, SPARE, rows, into(two_ref))
    sweep(two_ref, 0, SPARE + WIDE, size_y, into_result)
    sample_vertices(out_ref, cell_ref, sample_ref, table_ref)


def swept(wide, more, before, after, cells):
    _, planes, rows, _ = wide.shape
    size_x, size_y = planes - 2 * WIDE, rows - 2 * WIDE
    sources = cells.shape[1] // LANE
    stride = rows + 2 * SPARE
    return pl.pallas_call(
        sweep_kernel,
        name="sweeps",
        out_shape=(
            jax.ShapeDtypeStruct((3, size_x, size_y, LANE), F32),
            jax.ShapeDtypeStruct((sources * 9, LANE), F32),
        ),
        in_specs=[VMEM] * 5,
        out_specs=(VMEM, VMEM),
        scratch_shapes=[
            pltpu.VMEM((5, planes, 2 * stride, LANE), F32),
            pltpu.VMEM((3, planes, 2 * stride, LANE), F32),
            pltpu.VMEM((4, planes, 2 * stride, LANE), F32),
            pltpu.VMEM((6 * size_x * size_y // 2, 2 * LANE), BF16),
        ],
        compiler_params=pltpu.CompilerParams(vmem_limit_bytes=40 << 20),
        cost_estimate=pl.CostEstimate(flops=10 << 40, bytes_accessed=1 << 20, transcendentals=0),
    )(wide, more, before, after, cells)


def both_ways(down, up, axis):
    count = lax.axis_size(axis)
    above = lax.ppermute(down, axis, [((i + 1) % count, i) for i in range(count)])
    below = lax.ppermute(up, axis, [(i, (i + 1) % count) for i in range(count)])
    return below, above


def per_device(tri_geom, send_index, near_index, return_cell, velocity):
    size_x, size_y, size_z = near_index.shape
    group_x, group_y = lax.axis_size("gx"), lax.axis_size("gy")
    vel_low, vel_high = velocity[:, :WIDE], velocity[:, WIDE:]
    vel_below, vel_above = both_ways(vel_low, vel_high, "gx")
    mid_z = (lax.axis_index("gz") * size_z + size_z // 2).astype(F32)
    mid_x, mid_y = 0.5 * group_x * size_x, 0.5 * group_y * size_y
    outgoing = send_tables(tri_geom, send_index, jnp.stack([jnp.float32(mid_x), jnp.float32(mid_y), mid_z]))
    arrived = lax.all_to_all(
        outgoing.reshape(-1, 5 * LANE), ("gx", "gy"), split_axis=0, concat_axis=0, tiled=True
    ).reshape(-1, LANE)
    vel_down, vel_up = pack_y(vel_low, vel_high, vel_below, vel_above)
    vel_under, vel_over = both_ways(vel_down, vel_up, "gy")
    own_x = (lax.axis_index("gx") * size_x + size_x // 2).astype(F32) - mid_x
    own_y = (lax.axis_index("gy") * size_y + size_y // 2).astype(F32) - mid_y
    indicator, low, high = cell_fields(arrived, near_index, jnp.stack([own_x, own_y, jnp.float32(0.0)]))
    below, above = both_ways(low, high, "gx")
    down, up = pack_y(low, high, below, above)
    under, over = both_ways(down, up, "gy")
    wide, *begun = pack_z(0, (vel_low, vel_high, vel_below, vel_above, vel_under, vel_over))
    more, down, up = pack_z(3, (low, high, below, above, under, over), begun)
    before, after = both_ways(down, up, "gz")
    current, samples = swept(wide, more, before, after, return_cell)
    returned = lax.all_to_all(
        samples.reshape(-1, 9 * LANE), ("gx", "gy"), split_axis=0, concat_axis=0, tiled=True
    ).reshape(-1, LANE)
    return (current, indicator, bring_home(returned, send_index, tri_geom.shape[1]))


def solution(mesh):
    placed = (
        P(None, ("gx", "gy", "gz")),
        P(("gx", "gy", "gz"), None),
        P("gx", "gy", "gz"),
        P(None, ("gx", "gy", "gz")),
        P(None, "gx", "gy", "gz"),
    )
    return jax.shard_map(
        per_device,
        mesh=mesh,
        in_specs=placed,
        out_specs=(P(None, "gx", "gy", "gz"), P("gx", "gy", "gz"), P(None, ("gx", "gy", "gz"))),
        check_vma=False,
    )
```
